128 devices in a mesh: dp: 8 (over z, core), seq: 16 (over y, x).
Axes of the slice: x: 4, y: 4, z: 4, core: 2. Of those that a mesh axis runs over, the one named last changes fastest.
Arguments:
- hidden: bfloat16 [8, 2048, 1536], P('dp', 'seq'), may hold values from -6 to 6
- segments: int32 [8, 2048], P('dp', 'seq'), may hold values from 0 to 3, as said below
- pre_gain: bfloat16 [1536], P(('dp', 'seq')), may hold values from 0.5 to 1.5
- w_in: bfloat16 [1536, 6448], P(('dp', 'seq')), may hold values from -0.15625 to 0.15625
- conv_weight: bfloat16 [4, 3328], P(None, ('dp', 'seq')), may hold values from -3 to 3
- conv_bias: bfloat16 [3328], P(('dp', 'seq')), may hold values from -3 to 3
- dt_bias: float32 [48], replicated, may hold values from -8 to -5
- a_log: float32 [48], replicated, may hold values from -1 to 3
- d_skip: float32 [48], replicated, may hold values from 0.5 to 1.5
- gate_gain: bfloat16 [3072], P(('dp', 'seq')), may hold values from 0.5 to 1.5
- w_out: bfloat16 [3072, 1536], P(('dp', 'seq')), may hold values from -0.109375 to 0.109375
- grad_out: bfloat16 [8, 2048, 1536], P('dp', 'seq'), may hold values from -6 to 6
Outputs:
- block_out: bfloat16 [8, 2048, 1536], P('dp', 'seq')
- grad_hidden: bfloat16 [8, 2048, 1536], P('dp', 'seq')
- grad_pre_gain: float32 [1536], P(('dp', 'seq'))
- grad_w_in: float32 [1536, 6448], P(('dp', 'seq'))
- grad_conv_weight: float32 [4, 3328], P(None, ('dp', 'seq'))
- grad_conv_bias: float32 [3328], P(('dp', 'seq'))
- grad_dt_bias: float32 [48], replicated
- grad_a_log: float32 [48], replicated
- grad_d_skip: float32 [48], replicated
- grad_gate_gain: float32 [3072], P(('dp', 'seq'))
- grad_w_out: float32 [3072, 1536], P(('dp', 'seq'))
The draws below stay inside these ranges and needn't reach their ends.
Inputs may be any that keep to these rules, and one draw needn't show every extreme that they name: `segments`: in every sequence the segment numbers rise from 0 to 3 along the positions, one number per document; every document has 102 or more positions and exactly one has 1024.
All inputs are finite; a program needn't handle non-finite values.
Results may differ from the reference program's by a relative error of at most 0.015.
Values may be sent and summed in bfloat16 or wider, within the bound.
No kernel may reach another device: no remote copies, remote signals or barrier semaphores. Data moves between devices by JAX's collectives and lax.ppermute only.
A program may use at most 192 MiB of HBM per device.

```python
from functools import partial
import jax
import jax.numpy as jnp
from jax import lax

D = 1536
INNER = 3072
HEADDIM = 64
STATE = 128
CONV = 4
SPAN = 256
DOCS = 4
HEADS = 48
CONV_CH = 3328
PROJ = 6448
SEQ_LEN = 2048
SEQS = 8
DOC_MOST = 1024
DOC_LEAST = 102


def draw_segments(key, part):
    key = jax.random.fold_in(key, 7)
    cut_key, slot_key = jax.random.split(key)
    spare_room = DOC_MOST - (DOCS - 1) * DOC_LEAST
    cut_points = jax.random.randint(cut_key, (SEQS, 2), 0, spare_room + 1)
    lower = jnp.minimum(cut_points[:, 0], cut_points[:, 1])
    upper = jnp.maximum(cut_points[:, 0], cut_points[:, 1])
    shorts = jnp.stack([DOC_LEAST + lower, DOC_LEAST + upper - lower, DOC_LEAST + spare_room - upper], axis=1)
    longest = jax.random.randint(slot_key, (SEQS,), 0, DOCS)
    columns = []
    for position in range(DOCS):
        before = shorts[:, min(position, DOCS - 2)]
        behind = shorts[:, max(position - 1, 0)]
        columns.append(jnp.where(position < longest, before, jnp.where(position == longest, DOC_MOST, behind)))
    lengths = jnp.stack(columns, axis=1).astype(jnp.int32)
    bounds = jnp.cumsum(lengths, axis=1)[:, :DOCS - 1]
    places = jnp.arange(SEQ_LEN, dtype=jnp.int32)
    return jnp.sum((places[None, :, None] >= bounds[:, None, :]).astype(jnp.int32), axis=2)


def block_scale(stream_key, shape, cuts, smallest, top_value):
    level, own = 1.0, jax.random.fold_in(stream_key, 6)
    for dim, parts in cuts:
        steps = jnp.exp(jax.random.uniform(jax.random.fold_in(own, dim), (parts,), jnp.float32, smallest / len(cuts), top_value / len(cuts)))
        level = level * jnp.repeat(steps, shape[dim] // parts).reshape([-1 if axis == dim else 1 for axis in range(len(shape))])
    return level


def gaussian(stream_key, shape, deviation, bound, cuts=(), kind=jnp.bfloat16):
    values = jax.random.normal(stream_key, shape, jnp.float32) * deviation
    if len(cuts) > 0:
        values = block_scale(stream_key, shape, cuts, -0.22, 0.18) * values
    return jnp.clip(values, min=-bound, max=bound).astype(kind)


def setup_inputs(seed: int = 0) -> dict:
    seeds = jax.random.split(jax.random.key(seed), 13)
    return {
        "hidden": gaussian(seeds[0], (SEQS, SEQ_LEN, D), 1.0, 6.0, ((0, 8), (1, 16))),
        "segments": draw_segments(jax.random.fold_in(seeds[12], 71), 0),
        "pre_gain": jnp.clip(1.0 + 0.1 * jax.random.normal(seeds[2], (D,), jnp.float32), 0.5, 1.5).astype(jnp.bfloat16),
        "w_in": gaussian(seeds[3], (D, PROJ), D ** -0.5, 0.15625, ((0, 128),)),
        "conv_weight": gaussian(seeds[4], (CONV, CONV_CH), CONV ** -0.5, 3.0, ((1, 128),)),
        "conv_bias": gaussian(seeds[5], (CONV_CH,), 0.5, 3.0, ((0, 128),)),
        "dt_bias": jnp.clip(jax.random.uniform(seeds[6], (HEADS,), jnp.float32, -8.0, -5.0), -8.0, -5.0),
        "a_log": jnp.clip(jax.random.uniform(seeds[7], (HEADS,), jnp.float32, -1.0, 3.0), -1.0, 3.0),
        "d_skip": jnp.clip(jax.random.uniform(seeds[8], (HEADS,), jnp.float32, 0.5, 1.5), 0.5, 1.5),
        "gate_gain": jnp.clip(1.0 + 0.1 * jax.random.normal(seeds[9], (INNER,), jnp.float32), 0.5, 1.5).astype(jnp.bfloat16),
        "w_out": gaussian(seeds[10], (INNER, D), INNER ** -0.5, 0.109375, ((0, 128),)),
        "grad_out": gaussian(seeds[11], (SEQS, SEQ_LEN, D), 1.0, 6.0, ((0, 8), (1, 16))),
    }


epsilon = 1e-05
highest = lax.Precision.HIGHEST

@jax.custom_vjp
def low(v):
    return lax.optimization_barrier(v.astype(jnp.bfloat16)).astype(jnp.float32)

@jax.custom_vjp
def low_back(v):
    return v

def low_keep(v):
    return (low(v), None)

def low_pass(kept, grad):
    return (grad,)

def back_keep(v):
    return (v, None)

def back_low(kept, grad):
    return (low(grad),)
low.defvjp(low_keep, low_pass)
low_back.defvjp(back_keep, back_low)

def norm_in(tokens, pre_gain):
    variance = lax.optimization_barrier(jnp.mean(tokens * tokens, axis=-1, keepdims=True))
    return tokens * lax.rsqrt(variance + epsilon) * pre_gain[None, :]

def conv_section(xbc_ext, conv_weight, conv_bias):
    length = xbc_ext.shape[0] - (CONV - 1)
    conv_sum = conv_bias[None, :] + conv_weight[0][None, :] * xbc_ext[0:length]
    for offset in range(1, CONV):
        conv_sum = conv_sum + conv_weight[offset][None, :] * xbc_ext[offset:offset + length]
    active = jax.nn.silu(conv_sum)
    x_heads = active[:, :INNER].reshape(length, HEADS, HEADDIM)
    b_rows = active[:, INNER:INNER + STATE]
    c_rows = active[:, INNER + STATE:]
    return (x_heads, b_rows, c_rows)

def decay_section(dt_raw, dt_bias, a_log):
    step_size = jax.nn.softplus(dt_raw + dt_bias[None, :])
    log_decay = -step_size * jnp.exp(a_log)[None, :]
    return (step_size, log_decay)

def intra_block(x_heads, step_size, log_decay, b_rows, c_rows, segment):
    cumulative = jnp.cumsum(log_decay, axis=0)
    length = segment.shape[0]
    places = jnp.arange(length)
    allowed = (segment[:, None] == segment[None, :]) & (places[:, None] >= places[None, :])
    spread = cumulative[:, None, :] - cumulative[None, :, :]
    kernel = jnp.exp(jnp.where(allowed[:, :, None], spread, -jnp.inf))
    scores = jnp.dot(c_rows, b_rows.T, precision=highest, preferred_element_type=jnp.float32)
    mixing = scores[:, :, None] * kernel * step_size[None, :, :]
    y_inner = jnp.einsum('tsh,shp->thp', mixing, x_heads, precision=highest)
    same_end = (segment == segment[-1])[:, None]
    to_end = jnp.exp(jnp.where(same_end, cumulative[-1][None, :] - cumulative, -jnp.inf))
    weighted = (to_end * step_size)[:, :, None] * x_heads
    local_state = jnp.einsum('shp,sn->hpn', weighted, b_rows, precision=highest)
    whole_decay = jnp.exp(cumulative[-1]) * (segment[0] == segment[-1]).astype(jnp.float32)
    entry_decay = jnp.exp(cumulative) * (segment == segment[0]).astype(jnp.float32)[:, None]
    return (y_inner, local_state, whole_decay, entry_decay)

def sequence_ssd(x_heads, step_size, log_decay, b_rows, c_rows, segment):
    blocks = SEQ_LEN // SPAN

    def by_block(member):
        return member.reshape((blocks, SPAN) + member.shape[1:])

    def advance(running, pieces):
        head_state, previous = running
        x_part, step_part, decay_part, b_part, c_part, seg_part = pieces
        y_inner, local_state, whole_decay, entry_decay = intra_block(x_part, step_part, decay_part, b_part, c_part, seg_part)
        carried = (seg_part[0] == previous).astype(jnp.float32)
        from_state = jnp.einsum('tn,hpn->thp', c_part, head_state, precision=highest)
        y_part = y_inner + (entry_decay * carried)[:, :, None] * from_state
        new_state = local_state + (whole_decay * carried)[:, None, None] * head_state
        return ((new_state, seg_part[-1]), y_part)
    initial = (jnp.zeros((HEADS, HEADDIM, STATE), jnp.float32), jnp.array(-1, jnp.int32))
    pieces = (by_block(x_heads), by_block(step_size), by_block(log_decay), by_block(b_rows), by_block(c_rows), by_block(segment))
    ignored, outputs = lax.scan(jax.checkpoint(advance), initial, pieces)
    return outputs.reshape(SEQ_LEN, HEADS, HEADDIM)

def gated_finish(y_ssd, x_heads, z_gate, d_skip, gate_gain):
    y_full = (y_ssd + d_skip[None, :, None] * x_heads).reshape(-1, INNER)
    gated = y_full * jax.nn.silu(z_gate)
    variance = lax.optimization_barrier(jnp.mean(gated * gated, axis=-1, keepdims=True))
    return gated * lax.rsqrt(variance + epsilon) * gate_gain[None, :]

def forward(tokens, pre_gain, w_in, conv_weight, conv_bias, dt_bias, a_log, d_skip, gate_gain, w_out, segment):
    normed_in = low(norm_in(tokens, pre_gain))
    projected = low_back(low(jnp.dot(normed_in, w_in, precision=highest, preferred_element_type=jnp.float32)))
    z_gate = projected[:, :INNER]
    conv_in = projected[:, INNER:INNER + CONV_CH]
    dt_raw = projected[:, INNER + CONV_CH:]
    xbc_ext = jnp.concatenate([jnp.zeros((CONV - 1, CONV_CH), jnp.float32), conv_in], axis=0)
    x_heads, b_rows, c_rows = conv_section(xbc_ext, conv_weight, conv_bias)
    step_size, log_decay = decay_section(dt_raw, dt_bias, a_log)
    y_ssd = sequence_ssd(x_heads, step_size, log_decay, b_rows, c_rows, segment)
    normed_out = low(gated_finish(y_ssd, x_heads, z_gate, d_skip, gate_gain))
    return jnp.dot(normed_out, w_out, precision=highest, preferred_element_type=jnp.float32) + tokens

def reference(hidden, segments, pre_gain, w_in, conv_weight, conv_bias, dt_bias, a_log, d_skip, gate_gain, w_out, grad_out):
    params = (pre_gain.astype(jnp.float32), w_in.astype(jnp.float32), conv_weight.astype(jnp.float32), conv_bias.astype(jnp.float32), dt_bias.astype(jnp.float32), a_log.astype(jnp.float32), d_skip.astype(jnp.float32), gate_gain.astype(jnp.float32), w_out.astype(jnp.float32))

    def one_sequence(totals, pieces):
        tokens, segment, cotangent = pieces
        block_value, pullback = jax.vjp(partial(forward, segment=segment), tokens.astype(jnp.float32), *params)
        gradients = pullback(cotangent.astype(jnp.float32))
        totals = tuple((running + extra for running, extra in zip(totals, gradients[1:])))
        return (totals, (block_value.astype(jnp.bfloat16), gradients[0].astype(jnp.bfloat16)))
    initial = tuple((jnp.zeros_like(member) for member in params))
    totals, outputs = lax.scan(one_sequence, initial, (hidden, segments, grad_out))
    return (outputs[0], outputs[1], totals[0], totals[1], totals[2], totals[3], totals[4], totals[5], totals[6], totals[7], totals[8])
```

```python
import jax
import jax.numpy as jnp
from jax import lax
from jax.experimental import pallas as pl
from jax.experimental.pallas import tpu as pltpu
from jax.sharding import PartitionSpec as P

D = 1536
INNER = 3072
STATE = 128
CONV = 4
HEADS = 48
CONV_CH = 3328
CHUNK = 128
OWN = 3
WIDE = 192
PAD = 768
low = jnp.bfloat16
f32 = jnp.float32


def mm(a, b, dims=((1,), (0,))):
    return lax.dot_general(a, b, (dims, ((), ())), preferred_element_type=f32)


NT = ((1,), (1,))
TN = ((0,), (0,))


def per_head(parts):
    lane = lax.broadcasted_iota(jnp.int32, (1, WIDE), 1)
    return jnp.where(lane < 64, parts[0], jnp.where(lane < 128, parts[1], parts[2]))


def stacked(a):
    lane = lax.broadcasted_iota(jnp.int32, a.shape, 1)
    zero = jnp.zeros_like(a)
    return jnp.concatenate(
        [jnp.where((lane >= 64 * h) & (lane < 64 * h + 64), a, zero) for h in range(OWN)], axis=0
    )


def running(a, back):
    lane = lax.broadcasted_iota(jnp.int32, a.shape, 1)
    step = 1
    while step < CHUNK:
        if back:
            a = a + jnp.where(lane < CHUNK - step, pltpu.roll(a, CHUNK - step, 1), 0.0)
        else:
            a = a + jnp.where(lane >= step, pltpu.roll(a, step, 1), 0.0)
        step *= 2
    return a


def chunk_terms(zdt, rows, head_ref):
    raw = zdt[:, 128:256].T[64:72]
    v = raw + head_ref[0]
    ea = jnp.exp(head_ref[1])
    step = jnp.maximum(v, 0.0) + jnp.log1p(jnp.exp(-jnp.abs(v)))
    ld = -step * ea
    cum = running(ld, False)
    total = cum[:, CHUNK - 1 : CHUNK]
    seg = rows[0:1]
    before = rows[1:2, 0:1]
    last = seg[:, CHUNK - 1 : CHUNK]
    entry = jnp.exp(cum) * (seg == before).astype(f32)
    to_end = jnp.exp(total - cum) * (seg == last).astype(f32)
    whole = jnp.exp(total) * (last == before).astype(f32)
    pack = jnp.concatenate(
        [cum, entry, to_end * step, rows, jnp.zeros((CHUNK - 32, CHUNK), f32)], axis=0
    )
    cols = pack.T
    t = lax.broadcasted_iota(jnp.int32, (CHUNK, CHUNK), 0)
    s = lax.broadcasted_iota(jnp.int32, (CHUNK, CHUNK), 1)
    barred = jnp.where((t >= s) & (cols[:, 24:25] == seg), 0.0, -1e30)
    return v, ea, step, ld, cum, to_end, whole, cols, barred


def convolved(ext_ref, conv_ref):
    pre = conv_ref[CONV : CONV + 1, :]
    for k in range(CONV):
        pre = pre + conv_ref[k : k + 1, :] * ext_ref[pl.ds(5 + k, CHUNK), :]
    return pre


def decays(cols, cum, barred, h):
    return jnp.exp(cols[:, h : h + 1] - cum[h : h + 1] + barred)


def forward_kernel(
    proj_ref, rows_ref, conv_ref, head_ref, skip_ref, y_ref, gated_ref, kept_ref, ext_ref, state_ref
):
    first = pl.program_id(0) == 0

    @pl.when(first)
    def _():
        ext_ref[0:8, :] = jnp.zeros((8, 512), f32)
        state_ref[...] = jnp.zeros_like(state_ref)

    @pl.when(jnp.logical_not(first))
    def _():
        ext_ref[0:8, :] = ext_ref[CHUNK : CHUNK + 8, :]

    ext_ref[8 : CHUNK + 8, :] = proj_ref[:, 256:PAD].astype(f32)
    zdt = proj_ref[:, 0:256].astype(f32)
    pre = convolved(ext_ref, conv_ref)
    act = pre * jax.nn.sigmoid(pre)
    x = act[:, :WIDE]
    b_low = act[:, 256:384].astype(low)
    c_low = act[:, 384:512].astype(low)
    v, ea, step, ld, cum, to_end, whole, cols, barred = chunk_terms(zdt, rows_ref[...], head_ref)
    scores = mm(c_low, b_low, NT)
    mixing = jnp.concatenate(
        [
            (scores * decays(cols, cum, barred, h) * step[h : h + 1]).astype(low)
            for h in range(OWN)
        ],
        axis=1,
    )
    state = state_ref[...]
    kept_ref[0] = state
    entry = per_head([cols[:, 8 + h : 9 + h] for h in range(OWN)])
    y = mm(mixing, stacked(x.astype(low))) + entry * mm(c_low, state.astype(low))
    leaving = per_head([cols[:, 16 + h : 17 + h] for h in range(OWN)])
    state_ref[...] = per_head([whole[h : h + 1] for h in range(OWN)]) * state + mm(
        b_low, (leaving * x).astype(low), TN
    )
    y = y + skip_ref[...] * x
    z = zdt[:, :WIDE]
    y_ref[...] = y
    gated_ref[...] = (y * z * jax.nn.sigmoid(z)).astype(low)


def backward_kernel(
    proj_ref,
    before_ref,
    rows_ref,
    conv_ref,
    head_ref,
    skip_ref,
    y_ref,
    u_ref,
    kept_ref,
    d_proj_ref,
    conv_grad_ref,
    head_grad_ref,
    skip_grad_ref,
    ext_ref,
    later_ref,
    state_ref,
):
    step_id = pl.program_id(0)
    count = pl.num_programs(0)

    @pl.when(step_id == 0)
    def _():
        later_ref[CHUNK : CHUNK + 8, :] = jnp.zeros((8, 512), f32)
        state_ref[...] = jnp.zeros_like(state_ref)
        conv_grad_ref[...] = jnp.zeros_like(conv_grad_ref)
        head_grad_ref[...] = jnp.zeros_like(head_grad_ref)
        skip_grad_ref[...] = jnp.zeros_like(skip_grad_ref)

    @pl.when(step_id > 0)
    def _():
        later_ref[CHUNK : CHUNK + 8, :] = later_ref[0:8, :]

    ahead = before_ref[8:16, 256:PAD].astype(f32)
    ext_ref[0:8, :] = jnp.where(step_id == count - 1, 0.0, ahead)
    conv_in = proj_ref[:, 256:PAD].astype(f32)
    ext_ref[8 : CHUNK + 8, :] = conv_in
    zdt = proj_ref[:, 0:256].astype(f32)
    pre = convolved(ext_ref, conv_ref)
    sig = jax.nn.sigmoid(pre)
    act = pre * sig
    slope = sig * (1.0 + pre * (1.0 - sig))
    x = act[:, :WIDE]
    x_low = x.astype(low)
    b_low = act[:, 256:384].astype(low)
    c_low = act[:, 384:512].astype(low)
    v, ea, step, ld, cum, to_end, whole, cols, barred = chunk_terms(zdt, rows_ref[...], head_ref)
    scores = mm(c_low, b_low, NT)

    z = zdt[:, :WIDE]
    z_sig = jax.nn.sigmoid(z)
    z_act = z * z_sig
    y = y_ref[...]
    d_gated = cols[:, 26:27] * u_ref[...] - cols[:, 27:28] * (y * z_act)
    dy = d_gated * z_act
    dz = d_gated * y * (z_sig * (1.0 + z * (1.0 - z_sig)))
    dy_low = dy.astype(low)

    state = kept_ref[0]
    state_low = state.astype(low)
    later = state_ref[...]
    later_low = later.astype(low)
    entry = per_head([cols[:, 8 + h : 9 + h] for h in range(OWN)])
    leaving = per_head([cols[:, 16 + h : 17 + h] for h in range(OWN)])
    wholes = per_head([whole[h : h + 1] for h in range(OWN)])

    x_stack = stacked(x_low)
    d_mixing = mm(dy_low, x_stack, NT)
    d_scores = jnp.zeros((CHUNK, CHUNK), f32)
    mixings = []
    flows = []
    d_steps = []
    for h in range(OWN):
        decay = decays(cols, cum, barred, h)
        stepped = decay * step[h : h + 1]
        mixing = scores * stepped
        mixings.append(mixing.astype(low))
        part = d_mixing[:, CHUNK * h : CHUNK * h + CHUNK]
        d_scores = d_scores + part * stepped
        flows.append((part * mixing).astype(low))
        d_steps.append(jnp.sum(part * scores * decay, axis=0, keepdims=True))
    d_scores = d_scores.astype(low)

    t = lax.broadcasted_iota(jnp.int32, (CHUNK, CHUNK), 0)
    s = lax.broadcasted_iota(jnp.int32, (CHUNK, CHUNK), 1)
    earlier = (t < s).astype(low)
    reach = mm(jnp.concatenate(flows, axis=0), earlier)
    inside = [
        jnp.sum(
            jnp.where(t >= s, reach[CHUNK * h : CHUNK * h + CHUNK], 0.0), axis=0, keepdims=True
        )
        for h in range(OWN)
    ]
    blank = jnp.zeros((8 - OWN, CHUNK), f32)

    from_later = mm(b_low, later_low)
    dx = (
        mm(jnp.concatenate(mixings, axis=0), stacked(dy_low), TN)
        + leaving * from_later
        + skip_ref[...] * dy
    )
    dy_entry = entry * dy
    dy_entry_low = dy_entry.astype(low)
    x_leaving = (leaving * x).astype(low)
    dc = mm(d_scores, b_low) + mm(dy_entry_low, state_low, NT)
    db = mm(d_scores, c_low, TN) + mm(x_leaving, later_low, NT)

    row_head = lax.broadcasted_iota(jnp.int32, (8, WIDE), 0)
    lane = lax.broadcasted_iota(jnp.int32, (8, WIDE), 1)
    by_head = ((lane >= 64 * row_head) & (lane < 64 * row_head + 64)).astype(low)
    xv = mm(by_head, (x * from_later).astype(low), NT)
    row_state = mm(by_head, (dy_entry * mm(c_low, state_low)).astype(low), NT)
    overlap = jnp.sum(mm(by_head, (later * state).astype(low), NT), axis=1, keepdims=True)
    ended = to_end * xv
    col_state = ended * step
    d_step = jnp.concatenate(d_steps + [blank], axis=0) + ended
    d_ld = (
        jnp.concatenate(inside + [blank], axis=0)
        + running(row_state, True)
        + (running(col_state, False) - col_state)
        + whole * overlap
    )
    d_dt = (d_step - d_ld * ea) * jax.nn.sigmoid(v)
    head_grad_ref[0] += d_dt
    head_grad_ref[1] += d_ld * ld
    skip_grad_ref[...] += jnp.sum((dy * x).reshape(16, 8, WIDE), axis=0)
    state_ref[...] = wholes * later + mm(c_low, dy_entry_low, TN)

    later_ref[0:CHUNK, 0:WIDE] = dx * slope[:, :WIDE]
    later_ref[0:CHUNK, WIDE:256] = jnp.zeros((CHUNK, 256 - WIDE), f32)
    later_ref[0:CHUNK, 256:384] = db * slope[:, 256:384]
    later_ref[0:CHUNK, 384:512] = dc * slope[:, 384:512]
    d_conv_in = jnp.zeros((CHUNK, 512), f32)
    for k in range(CONV):
        moved = later_ref[pl.ds(CONV - 1 - k, CHUNK), :]
        d_conv_in = d_conv_in + conv_ref[k : k + 1, :] * moved
        conv_grad_ref[k] += jnp.sum((moved * conv_in).reshape(16, 8, 512), axis=0)
        if k == CONV - 1:
            conv_grad_ref[CONV] += jnp.sum(moved.reshape(16, 8, 512), axis=0)

    turned = jnp.concatenate(
        [jnp.zeros((64, CHUNK), f32), d_dt, jnp.zeros((56, CHUNK), f32)], axis=0
    ).T
    d_proj_ref[:, 0:128] = dz[:, 0:128].astype(low)
    d_proj_ref[:, 128:256] = jnp.concatenate([dz[:, 128:WIDE], turned[:, 64:128]], axis=1).astype(
        low
    )
    d_proj_ref[:, 256:PAD] = d_conv_in.astype(low)


def ssd_forward(proj, rows, conv, heads, skip):
    length = proj.shape[0]
    chunks = length // CHUNK
    whole = lambda shape: pl.BlockSpec(shape, lambda i: (0,) * len(shape))
    return pl.pallas_call(
        forward_kernel,
        grid=(chunks,),
        in_specs=[
            pl.BlockSpec((CHUNK, PAD), lambda i: (i, 0)),
            pl.BlockSpec((8, CHUNK), lambda i: (0, i)),
            whole((8, 512)),
            whole((2, 8, CHUNK)),
            whole((1, WIDE)),
        ],
        out_specs=[
            pl.BlockSpec((CHUNK, WIDE), lambda i: (i, 0)),
            pl.BlockSpec((CHUNK, WIDE), lambda i: (i, 0)),
            pl.BlockSpec((1, STATE, WIDE), lambda i: (i, 0, 0)),
        ],
        out_shape=[
            jax.ShapeDtypeStruct((length, WIDE), f32),
            jax.ShapeDtypeStruct((length, WIDE), low),
            jax.ShapeDtypeStruct((chunks, STATE, WIDE), f32),
        ],
        scratch_shapes=[pltpu.VMEM((CHUNK + 8, 512), f32), pltpu.VMEM((STATE, WIDE), f32)],
        compiler_params=pltpu.CompilerParams(
            dimension_semantics=("arbitrary",), vmem_limit_bytes=32 * 1024 * 1024
        ),
        name="ssd_forward",
    )(proj, rows, conv, heads, skip)


def ssd_backward(proj, rows, conv, heads, skip, y, u, kept):
    length = proj.shape[0]
    chunks = length // CHUNK
    back = lambda i: chunks - 1 - i
    whole = lambda shape: pl.BlockSpec(shape, lambda i: (0,) * len(shape))
    return pl.pallas_call(
        backward_kernel,
        grid=(chunks,),
        in_specs=[
            pl.BlockSpec((CHUNK, PAD), lambda i: (back(i), 0)),
            pl.BlockSpec((16, PAD), lambda i: (jnp.maximum(back(i) * (CHUNK // 16) - 1, 0), 0)),
            pl.BlockSpec((8, CHUNK), lambda i: (0, back(i))),
            whole((8, 512)),
            whole((2, 8, CHUNK)),
            whole((1, WIDE)),
            pl.BlockSpec((CHUNK, WIDE), lambda i: (back(i), 0)),
            pl.BlockSpec((CHUNK, WIDE), lambda i: (back(i), 0)),
            pl.BlockSpec((1, STATE, WIDE), lambda i: (back(i), 0, 0)),
        ],
        out_specs=[
            pl.BlockSpec((CHUNK, PAD), lambda i: (back(i), 0)),
            whole((CONV + 1, 8, 512)),
            whole((2, 8, CHUNK)),
            whole((8, WIDE)),
        ],
        out_shape=[
            jax.ShapeDtypeStruct((length, PAD), low),
            jax.ShapeDtypeStruct((CONV + 1, 8, 512), f32),
            jax.ShapeDtypeStruct((2, 8, CHUNK), f32),
            jax.ShapeDtypeStruct((8, WIDE), f32),
        ],
        scratch_shapes=[
            pltpu.VMEM((CHUNK + 8, 512), f32),
            pltpu.VMEM((CHUNK + 8, 512), f32),
            pltpu.VMEM((STATE, WIDE), f32),
        ],
        compiler_params=pltpu.CompilerParams(
            dimension_semantics=("arbitrary",), vmem_limit_bytes=32 * 1024 * 1024
        ),
        name="ssd_backward",
    )(proj, proj, rows, conv, heads, skip, y, u, kept)

epsilon = 1e-05
BOTH = ("dp", "seq")


def columns_of(a):
    rows = a.shape[0]
    z = a[:, :INNER].reshape(rows, 16, WIDE)
    x = a[:, INNER : 2 * INNER].reshape(rows, 16, WIDE)
    bc = jnp.broadcast_to(a[:, None, 2 * INNER : 2 * INNER + 256], (rows, 16, 256))
    dt = a[:, 2 * INNER + 256 :].reshape(rows, 16, OWN)
    blank = lambda n: jnp.zeros((rows, 16, n), a.dtype)
    return jnp.concatenate([z, dt, blank(61), x, blank(64), bc], axis=2).transpose(1, 0, 2)


def padded(a):
    return jnp.concatenate(
        [a[:, :WIDE], jnp.zeros((a.shape[0], 64), a.dtype), a[:, WIDE:]], axis=1
    )


def block_order(back):
    pairs = [(f, (f % 8) * 16 + f // 8) for f in range(128)]
    return [(b, a) for a, b in pairs] if back else pairs


def local(
    hidden,
    segments,
    pre_gain,
    w_in,
    conv_weight,
    conv_bias,
    dt_bias,
    a_log,
    d_skip,
    gate_gain,
    w_out,
    grad_out,
):
    me = lax.axis_index("seq")
    row = lax.axis_index("dp")
    tokens = hidden[0].astype(f32)
    r0 = lax.rsqrt(jnp.mean(tokens * tokens, axis=-1, keepdims=True) + epsilon)
    hn = (tokens * r0).astype(low)
    hn_all = lax.all_gather(hn, "seq", axis=0, tiled=True)

    gain_in = pre_gain.astype(f32)[:, None]
    gain_out = gate_gain.astype(f32)[:, None]
    w_in_wide = w_in.astype(f32)
    w_out_wide = w_out.astype(f32)
    parts = columns_of((w_in_wide * gain_in).astype(low)).reshape(16 * 12, PAD)
    parts = lax.all_to_all(parts, "seq", 0, 0, tiled=True)
    blocks = lax.ppermute((w_out_wide * gain_out).astype(low), BOTH, block_order(False))
    weights = lax.all_gather(
        jnp.concatenate([parts, blocks.reshape(48, PAD)], axis=0), "dp", axis=0
    )
    w_own = weights[:, :192].reshape(D, PAD)
    w_out_own = weights[:, 192:].reshape(WIDE, D)

    small = jnp.concatenate(
        [conv_weight.reshape(-1), conv_bias, segments[0].astype(low)]
    )
    small = lax.all_to_all(
        jnp.broadcast_to(small[None], (128, small.shape[0])), BOTH, 0, 0, tiled=True
    ).astype(f32)
    conv_all = small[:, :130].reshape(128, 5, 26).transpose(1, 0, 2).reshape(5, CONV_CH)
    conv = jnp.concatenate(
        [lax.dynamic_slice_in_dim(conv_all, me * WIDE, WIDE, 1), conv_all[:, INNER:]], axis=1
    )
    conv = jnp.concatenate([padded(conv), jnp.zeros((3, 512), f32)], axis=0)
    segment = lax.dynamic_slice_in_dim(small[:, 130:], row * 16, 16, 0).reshape(1, 2048)
    before = jnp.concatenate([jnp.full((1, 1), -1.0, f32), segment[:, :-1]], axis=1)

    own = lambda a: lax.dynamic_slice_in_dim(a, me * OWN, OWN, 0)
    tall = lambda a: jnp.broadcast_to(jnp.pad(own(a), (0, 8 - OWN))[:, None], (8, CHUNK))
    heads = jnp.stack([tall(dt_bias), tall(a_log)])
    skip = jnp.repeat(own(d_skip), 64)[None]

    proj = jnp.dot(hn_all, w_own, preferred_element_type=f32).astype(low)
    rows = jnp.concatenate([segment, before, jnp.zeros((6, 2048), f32)], axis=0)
    y, gated, kept = ssd_forward(proj, rows, conv, heads, skip)

    cot_all = lax.all_gather(grad_out[0], "seq", axis=0, tiled=True)
    u = jnp.dot(cot_all, w_out_own.T, preferred_element_type=f32)
    gated_wide = gated.astype(f32)
    sums = jnp.stack([jnp.sum(gated_wide * gated_wide, axis=1), jnp.sum(u * gated_wide, axis=1)])
    sums = lax.all_to_all(
        jnp.broadcast_to(sums.reshape(1, 32, 128), (16, 32, 128)), "seq", 0, 0, tiled=True
    )
    sums = jnp.sum(sums, axis=0).reshape(2, 2048)
    r = lax.rsqrt(sums[0:1] / INNER + epsilon)
    c = r * r * r * (sums[1:2] / INNER)

    partial_out = jnp.dot(gated, w_out_own, preferred_element_type=f32).astype(low)
    total = lax.psum_scatter(partial_out, "seq", scatter_dimension=0, tiled=True)
    r_own = lax.dynamic_slice_in_dim(r[0], me * 128, 128, 0)
    block_out = (r_own[:, None] * total.astype(f32) + tokens).astype(low)

    rows = jnp.concatenate([segment, before, r, c, jnp.zeros((4, 2048), f32)], axis=0)
    d_proj, conv_grad, head_grad, skip_grad = ssd_backward(
        proj, rows, conv, heads, skip, y, u, kept
    )
    partial_in = lax.dot_general(
        d_proj, w_own, (((1,), (1,)), ((), ())), preferred_element_type=f32
    ).astype(low)
    v = lax.psum_scatter(partial_in, "seq", scatter_dimension=0, tiled=True).astype(f32)
    mean = jnp.mean(v * tokens, axis=-1, keepdims=True)
    grad_hidden = (
        grad_out[0].astype(f32) + r0 * v - tokens * (r0 * r0 * r0 * mean)
    ).astype(low)

    grad_in = lax.dot_general(
        hn_all, d_proj, (((0,), (0,)), ((), ())), preferred_element_type=f32
    )
    normed = (gated_wide * r.reshape(2048, 1)).astype(low)
    grad_out_w = lax.dot_general(
        normed, cot_all, (((0,), (0,)), ((), ())), preferred_element_type=f32
    )
    grads = jnp.concatenate(
        [grad_in.reshape(8, 192, PAD), grad_out_w.reshape(8, 48, PAD)], axis=1
    ).astype(low)
    grads = lax.psum_scatter(grads, "dp", scatter_dimension=0, tiled=False)
    g_parts = lax.all_to_all(grads[:192], "seq", 0, 0, tiled=True).reshape(16, 12, PAD)
    g_out = lax.ppermute(grads[192:].reshape(24, D), BOTH, block_order(True)).astype(f32)
    g_parts = g_parts.astype(f32).transpose(1, 0, 2)
    g_in = jnp.concatenate(
        [
            g_parts[:, :, :WIDE].reshape(12, INNER),
            g_parts[:, :, 256 : 256 + WIDE].reshape(12, INNER),
            jnp.sum(g_parts[:, :, 512:], axis=1),
            g_parts[:, :, WIDE : WIDE + OWN].reshape(12, HEADS),
        ],
        axis=1,
    )
    grad_w_in = gain_in * g_in
    grad_pre_gain = jnp.sum(w_in_wide * g_in, axis=1)
    grad_w_out = gain_out * g_out
    grad_gate_gain = jnp.sum(w_out_wide * g_out, axis=1)

    conv_own = jnp.sum(conv_grad, axis=1)
    conv_flat = jnp.zeros((5, CONV_CH), f32)
    conv_flat = lax.dynamic_update_slice(conv_flat, conv_own[:, 256:], (0, INNER))
    conv_flat = lax.dynamic_update_slice(conv_flat, conv_own[:, :WIDE], (0, me * WIDE))
    conv_flat = conv_flat.reshape(5, 128, 26).transpose(1, 0, 2).reshape(128, 130)
    head_own = jnp.concatenate(
        [
            jnp.sum(head_grad, axis=2)[:, :OWN].reshape(-1),
            jnp.sum(skip_grad, axis=0).reshape(OWN, 64).sum(axis=1),
        ]
    )
    tail = jnp.concatenate(
        [conv_flat, jnp.broadcast_to(head_own[None], (128, 9))], axis=1
    )
    tail = lax.all_to_all(tail, BOTH, 0, 0, tiled=True)
    conv_sum = jnp.sum(tail[:, :130], axis=0).reshape(5, 26)
    head_sum = jnp.sum(tail[:, 130:].reshape(8, 16, 3, OWN), axis=0)
    head_sum = head_sum.transpose(1, 0, 2).reshape(3, HEADS)
    return (
        block_out[None],
        grad_hidden[None],
        grad_pre_gain,
        grad_w_in,
        conv_sum[:CONV],
        conv_sum[CONV],
        head_sum[0],
        head_sum[1],
        head_sum[2],
        grad_gate_gain,
        grad_w_out,
    )


def solution(mesh):
    placed = (
        P("dp", "seq", None),
        P("dp", "seq"),
        P(BOTH),
        P(BOTH, None),
        P(None, BOTH),
        P(BOTH),
        P(),
        P(),
        P(),
        P(BOTH),
        P(BOTH, None),
        P("dp", "seq", None),
    )
    return jax.shard_map(
        local,
        mesh=mesh,
        in_specs=placed,
        out_specs=(
            P("dp", "seq", None),
            P("dp", "seq", None),
            P(BOTH),
            P(BOTH, None),
            P(None, BOTH),
            P(BOTH),
            P(),
            P(),
            P(),
            P(BOTH),
            P(BOTH, None),
        ),
        check_vma=False,
    )
```

```python
import jax
import jax.numpy as jnp
from jax import lax
from jax.experimental import pallas as pl
from jax.experimental.pallas import tpu as pltpu
from jax.sharding import PartitionSpec as P

D = 1536
INNER = 3072
STATE = 128
CONV = 4
HEADS = 48
CONV_CH = 3328
CHUNK = 128
GROUP = 4
BLOCK = CHUNK * GROUP
OWN = 3
WIDE = 192
PAD = 768
low = jnp.bfloat16
f32 = jnp.float32


def mm(a, b, dims=((1,), (0,))):
    return lax.dot_general(a, b, (dims, ((), ())), preferred_element_type=f32)


NT = ((1,), (1,))
TN = ((0,), (0,))


def per_head(parts):
    lane = lax.broadcasted_iota(jnp.int32, (1, WIDE), 1)
    return jnp.where(lane < 64, parts[0], jnp.where(lane < 128, parts[1], parts[2]))


def stacked(a):
    lane = lax.broadcasted_iota(jnp.int32, a.shape, 1)
    zero = jnp.zeros_like(a)
    return jnp.concatenate(
        [jnp.where((lane >= 64 * h) & (lane < 64 * h + 64), a, zero) for h in range(OWN)], axis=0
    )


def running(a, back):
    lane = lax.broadcasted_iota(jnp.int32, a.shape, 1)
    step = 1
    while step < CHUNK:
        if back:
            a = a + jnp.where(lane < CHUNK - step, pltpu.roll(a, CHUNK - step, 1), 0.0)
        else:
            a = a + jnp.where(lane >= step, pltpu.roll(a, step, 1), 0.0)
        step *= 2
    return a


def part(a, j):
    return a[CHUNK * j : CHUNK * (j + 1)]


def eight(a, j):
    return a[8 * j : 8 * (j + 1)]


def block_terms(zdt, rows_ref, head_ref):
    raw = jnp.concatenate([part(zdt, j)[:, 128:256].T[64:72] for j in range(GROUP)], axis=0)
    wide = lambda row: jnp.concatenate(
        [jnp.broadcast_to(rows_ref[j, row : row + 1, :], (8, CHUNK)) for j in range(GROUP)], axis=0
    )
    v = raw + head_ref[0]
    ea = jnp.exp(head_ref[1])
    step = jnp.maximum(v, 0.0) + jnp.log1p(jnp.exp(-jnp.abs(v)))
    ld = -step * ea
    cum = running(ld, False)
    total = cum[:, CHUNK - 1 : CHUNK]
    seg = wide(0)
    before = wide(1)[:, 0:1]
    last = seg[:, CHUNK - 1 : CHUNK]
    entry = jnp.exp(cum) * (seg == before).astype(f32)
    to_end = jnp.exp(total - cum) * (seg == last).astype(f32)
    whole = jnp.exp(total) * (last == before).astype(f32)
    leaving = to_end * step
    cols = []
    for j in range(GROUP):
        pack = [eight(cum, j), eight(entry, j), eight(leaving, j), rows_ref[j]]
        pack = jnp.concatenate(pack + [jnp.zeros((CHUNK - 32, CHUNK), f32)], axis=0)
        cols.append(pack.T)
    return v, ea, step, ld, cum, to_end, whole, cols


def barred(cols, seg):
    t = lax.broadcasted_iota(jnp.int32, (CHUNK, CHUNK), 0)
    s = lax.broadcasted_iota(jnp.int32, (CHUNK, CHUNK), 1)
    return jnp.where((t >= s) & (cols[:, 24:25] == seg), 0.0, -1e30)


def convolved(ext_ref, conv_ref):
    pre = conv_ref[CONV : CONV + 1, :]
    for k in range(CONV):
        pre = pre + conv_ref[k : k + 1, :] * ext_ref[pl.ds(5 + k, BLOCK), :]
    return pre


def forward_kernel(
    both_ref,
    w_ref,
    out_ref,
    rows_ref,
    conv_ref,
    head_ref,
    skip_ref,
    proj_ref,
    y_ref,
    gated_ref,
    u_ref,
    kept_ref,
    total_ref,
    sums_ref,
    ext_ref,
    state_ref,
):
    first = pl.program_id(0) == 0

    @pl.when(first)
    def _():
        ext_ref[0:8, :] = jnp.zeros((8, 512), f32)
        state_ref[...] = jnp.zeros_like(state_ref)

    @pl.when(jnp.logical_not(first))
    def _():
        ext_ref[0:8, :] = ext_ref[BLOCK : BLOCK + 8, :]

    proj_ref[...] = mm(both_ref[:, 0:D], w_ref[...]).astype(low)
    u_ref[...] = mm(both_ref[:, D : 2 * D], out_ref[...], NT)
    zdt = proj_ref[:, 0:256].astype(f32)
    ext_ref[8 : BLOCK + 8, :] = proj_ref[:, 256:PAD].astype(f32)
    pre = convolved(ext_ref, conv_ref)
    act = pre * jax.nn.sigmoid(pre)
    x = act[:, :WIDE]
    x_low = x.astype(low)
    b_low = act[:, 256:384].astype(low)
    c_low = act[:, 384:512].astype(low)
    v, ea, step, ld, cum, to_end, whole, cols = block_terms(zdt, rows_ref, head_ref)
    inner, local, entries, wholes = [], [], [], []
    for j in range(GROUP):
        col = cols[j]
        bar = barred(col, rows_ref[j, 0:1, :])
        scores = mm(part(c_low, j), part(b_low, j), NT)
        mixing = []
        for h in range(OWN):
            i = 8 * j + h
            decay = jnp.exp(col[:, h : h + 1] - cum[i : i + 1] + bar)
            mixing.append((scores * decay * step[i : i + 1]).astype(low))
        inner.append(mm(jnp.concatenate(mixing, axis=1), stacked(part(x_low, j))))
        leaving = per_head([col[:, 16 + h : 17 + h] for h in range(OWN)])
        local.append(mm(part(b_low, j), (leaving * part(x, j)).astype(low), TN))
        entries.append(per_head([col[:, 8 + h : 9 + h] for h in range(OWN)]))
        wholes.append(per_head([whole[8 * j + h : 8 * j + h + 1] for h in range(OWN)]))
    state = state_ref[...]
    ys = []
    for j in range(GROUP):
        kept_ref[j] = state
        ys.append(inner[j] + entries[j] * mm(part(c_low, j), state.astype(low)))
        state = wholes[j] * state + local[j]
    state_ref[...] = state
    y = jnp.concatenate(ys, axis=0) + skip_ref[...] * x
    z = zdt[:, :WIDE]
    gated = y * z * jax.nn.sigmoid(z)
    gated_low = gated.astype(low)
    y_ref[...] = y
    gated_ref[...] = gated_low
    total_ref[...] = mm(gated_low, out_ref[...]).astype(low)
    ones = jnp.ones((8, WIDE), low)
    squares = mm(ones, (gated * gated).astype(low), NT)
    products = mm(ones, (gated * u_ref[...]).astype(low), NT)
    row = lax.broadcasted_iota(jnp.int32, (8, BLOCK), 0)
    sums_ref[...] = jnp.where(row == 0, squares, products)


def backward_kernel(
    place_ref,
    proj_ref,
    before_ref,
    w_ref,
    cot_ref,
    rows_ref,
    conv_ref,
    head_ref,
    skip_ref,
    y_ref,
    gated_ref,
    u_ref,
    kept_ref,
    d_proj_ref,
    top_ref,
    bottom_ref,
    out_grad_ref,
    sums_ref,
    ext_ref,
    later_ref,
    state_ref,
    conv_grad_ref,
    head_grad_ref,
    skip_grad_ref,
):
    step_id = pl.program_id(0)
    count = pl.num_programs(0)

    @pl.when(step_id == 0)
    def _():
        later_ref[BLOCK : BLOCK + 8, :] = jnp.zeros((8, 512), f32)
        state_ref[...] = jnp.zeros_like(state_ref)
        conv_grad_ref[...] = jnp.zeros_like(conv_grad_ref)
        head_grad_ref[...] = jnp.zeros_like(head_grad_ref)
        skip_grad_ref[...] = jnp.zeros_like(skip_grad_ref)
        out_grad_ref[...] = jnp.zeros_like(out_grad_ref)

    @pl.when(step_id > 0)
    def _():
        later_ref[BLOCK : BLOCK + 8, :] = later_ref[0:8, :]

    ahead = before_ref[8:16, 256:PAD].astype(f32)
    ext_ref[0:8, :] = jnp.where(step_id == count - 1, 0.0, ahead)
    conv_in = proj_ref[:, 256:PAD].astype(f32)
    ext_ref[8 : BLOCK + 8, :] = conv_in
    zdt = proj_ref[:, 0:256].astype(f32)
    pre = convolved(ext_ref, conv_ref)
    sig = jax.nn.sigmoid(pre)
    act = pre * sig
    slope = sig * (1.0 + pre * (1.0 - sig))
    x = act[:, :WIDE]
    x_low = x.astype(low)
    b_low = act[:, 256:384].astype(low)
    c_low = act[:, 384:512].astype(low)
    v, ea, step, ld, cum, to_end, whole, cols = block_terms(zdt, rows_ref, head_ref)

    z = zdt[:, :WIDE]
    z_sig = jax.nn.sigmoid(z)
    z_act = z * z_sig
    y = y_ref[...]
    r_col = jnp.concatenate([c[:, 26:27] for c in cols], axis=0)
    c_col = jnp.concatenate([c[:, 27:28] for c in cols], axis=0)
    d_gated = r_col * u_ref[...] - c_col * (y * z_act)
    dy = d_gated * z_act
    dz = d_gated * y * (z_sig * (1.0 + z * (1.0 - z_sig)))
    dy_low = dy.astype(low)
    normed = (gated_ref[...].astype(f32) * r_col).astype(low)
    out_grad_ref[...] += mm(normed, cot_ref[...], TN)

    t = lax.broadcasted_iota(jnp.int32, (CHUNK, CHUNK), 0)
    s = lax.broadcasted_iota(jnp.int32, (CHUNK, CHUNK), 1)
    earlier = (t < s).astype(low)
    blank = jnp.zeros((8 - OWN, CHUNK), f32)
    row_head = lax.broadcasted_iota(jnp.int32, (8, WIDE), 0)
    lane = lax.broadcasted_iota(jnp.int32, (8, WIDE), 1)
    by_head = ((lane >= 64 * row_head) & (lane < 64 * row_head + 64)).astype(low)

    dx_in, d_scores_all, d_steps_all, inside_all = [], [], [], []
    entries, leavings, wholes, to_state, dy_entries = [], [], [], [], []
    for j in range(GROUP):
        col = cols[j]
        bar = barred(col, rows_ref[j, 0:1, :])
        scores = mm(part(c_low, j), part(b_low, j), NT)
        d_mixing = mm(part(dy_low, j), stacked(part(x_low, j)), NT)
        d_scores = jnp.zeros((CHUNK, CHUNK), f32)
        mixings, flows, d_steps = [], [], []
        for h in range(OWN):
            i = 8 * j + h
            decay = jnp.exp(col[:, h : h + 1] - cum[i : i + 1] + bar)
            stepped = decay * step[i : i + 1]
            mixing = scores * stepped
            mixings.append(mixing.astype(low))
            d_mix = d_mixing[:, CHUNK * h : CHUNK * h + CHUNK]
            d_scores = d_scores + d_mix * stepped
            flows.append((d_mix * mixing).astype(low))
            d_steps.append(jnp.sum(d_mix * scores * decay, axis=0, keepdims=True))
        reach = mm(jnp.concatenate(flows, axis=0), earlier)
        inside = [
            jnp.sum(jnp.where(t >= s, part(reach, h), 0.0), axis=0, keepdims=True)
            for h in range(OWN)
        ]
        d_scores_all.append(d_scores.astype(low))
        d_steps_all += d_steps + [blank]
        inside_all += inside + [blank]
        dx_in.append(mm(jnp.concatenate(mixings, axis=0), stacked(part(dy_low, j)), TN))
        entry = per_head([col[:, 8 + h : 9 + h] for h in range(OWN)])
        dy_entry = entry * part(dy, j)
        dy_entries.append(dy_entry)
        to_state.append(mm(part(c_low, j), dy_entry.astype(low), TN))
        leavings.append(per_head([col[:, 16 + h : 17 + h] for h in range(OWN)]))
        wholes.append(per_head([whole[8 * j + h : 8 * j + h + 1] for h in range(OWN)]))

    laters = [None] * GROUP
    later = state_ref[...]
    for j in reversed(range(GROUP)):
        laters[j] = later
        later = wholes[j] * later + to_state[j]
    state_ref[...] = later

    xv, row_state, overlap, dxs, dbs, dcs = [], [], [], [], [], []
    for j in range(GROUP):
        bj, cj, xj = part(b_low, j), part(c_low, j), part(x, j)
        state_low = kept_ref[j].astype(low)
        later_low = laters[j].astype(low)
        from_later = mm(bj, later_low)
        dxs.append(dx_in[j] + leavings[j] * from_later)
        x_leaving = (leavings[j] * xj).astype(low)
        d_scores = d_scores_all[j]
        dcs.append(mm(d_scores, bj) + mm(dy_entries[j].astype(low), state_low, NT))
        dbs.append(mm(d_scores, cj, TN) + mm(x_leaving, later_low, NT))
        xv.append(mm(by_head, (xj * from_later).astype(low), NT))
        row_state.append(mm(by_head, (dy_entries[j] * mm(cj, state_low)).astype(low), NT))
        both = mm(by_head, (laters[j] * kept_ref[j]).astype(low), NT)
        overlap.append(jnp.sum(both, axis=1, keepdims=True))
    stack = lambda a: jnp.concatenate(a, axis=0)
    ended = to_end * stack(xv)
    col_state = ended * step
    d_step = stack(d_steps_all) + ended
    d_ld = (
        stack(inside_all)
        + running(stack(row_state), True)
        + (running(col_state, False) - col_state)
        + whole * stack(overlap)
    )
    d_dt = (d_step - d_ld * ea) * jax.nn.sigmoid(v)
    head_grad_ref[0] += sum([eight(d_dt, j) for j in range(GROUP)])
    head_grad_ref[1] += sum([eight(d_ld * ld, j) for j in range(GROUP)])
    skip_grad_ref[...] += jnp.sum((dy * x).reshape(BLOCK // 8, 8, WIDE), axis=0)

    dx = stack(dxs) + skip_ref[...] * dy
    later_ref[0:BLOCK, 0:WIDE] = dx * slope[:, :WIDE]
    later_ref[0:BLOCK, WIDE:256] = jnp.zeros((BLOCK, 256 - WIDE), f32)
    later_ref[0:BLOCK, 256:384] = stack(dbs) * slope[:, 256:384]
    later_ref[0:BLOCK, 384:512] = stack(dcs) * slope[:, 384:512]
    d_conv_in = jnp.zeros((BLOCK, 512), f32)
    for k in range(CONV):
        moved = later_ref[pl.ds(CONV - 1 - k, BLOCK), :]
        d_conv_in = d_conv_in + conv_ref[k : k + 1, :] * moved
        conv_grad_ref[k] += jnp.sum((moved * conv_in).reshape(BLOCK // 8, 8, 512), axis=0)
        if k == CONV - 1:
            conv_grad_ref[CONV] += jnp.sum(moved.reshape(BLOCK // 8, 8, 512), axis=0)

    turned = []
    for j in range(GROUP):
        tall = [jnp.zeros((64, CHUNK), f32), eight(d_dt, j), jnp.zeros((56, CHUNK), f32)]
        turned.append(jnp.concatenate(tall, axis=0).T)
    d_proj_ref[:, 0:128] = dz[:, 0:128].astype(low)
    d_proj_ref[:, 128:256] = jnp.concatenate(
        [dz[:, 128:WIDE], stack(turned)[:, 64:128]], axis=1
    ).astype(low)
    d_proj_ref[:, 256:PAD] = d_conv_in.astype(low)

    row = count - 1 - step_id
    my_x, my_y = place_ref[0], place_ref[1]
    up = lax.rem(row - my_y + 4, 4)
    for j in range(GROUP):
        given = mm(d_proj_ref[CHUNK * j : CHUNK * (j + 1), :], w_ref[...], NT).astype(low)
        top_ref[up, j] = given[:64]
        bottom_ref[lax.rem(j - my_x + 4, 4), row] = given[64:]

    @pl.when(step_id == count - 1)
    def _():
        sums_ref[...] = jnp.zeros_like(sums_ref)
        for k in range(CONV + 1):
            sums_ref[k : k + 1, :] = jnp.sum(conv_grad_ref[k], axis=0, keepdims=True)
        sums_ref[5:6, 0:WIDE] = jnp.sum(skip_grad_ref[...], axis=0, keepdims=True)
        place = lax.broadcasted_iota(jnp.int32, (8, CHUNK), 1)
        bias = jnp.sum(head_grad_ref[0], axis=1, keepdims=True)
        rate = jnp.sum(head_grad_ref[1], axis=1, keepdims=True)
        sums_ref[8:16, 0:CHUNK] = jnp.where(place == 0, bias, jnp.where(place == 1, rate, 0.0))


def ssd_forward(both, w, w_out, rows, conv, heads, skip):
    length = both.shape[0]
    steps = length // BLOCK
    whole = lambda shape: pl.BlockSpec(shape, lambda i: (0,) * len(shape))
    here = lambda width: pl.BlockSpec((BLOCK, width), lambda i: (i, 0))
    return pl.pallas_call(
        forward_kernel,
        grid=(steps,),
        in_specs=[
            here(2 * D),
            whole((D, PAD)),
            whole((WIDE, D)),
            pl.BlockSpec((GROUP, 8, CHUNK), lambda i: (i, 0, 0)),
            whole((8, 512)),
            whole((2, 8 * GROUP, CHUNK)),
            whole((1, WIDE)),
        ],
        out_specs=[
            here(PAD),
            here(WIDE),
            here(WIDE),
            here(WIDE),
            pl.BlockSpec((GROUP, STATE, WIDE), lambda i: (i, 0, 0)),
            here(D),
            pl.BlockSpec((8, BLOCK), lambda i: (0, i)),
        ],
        out_shape=[
            jax.ShapeDtypeStruct((length, PAD), low),
            jax.ShapeDtypeStruct((length, WIDE), f32),
            jax.ShapeDtypeStruct((length, WIDE), low),
            jax.ShapeDtypeStruct((length, WIDE), f32),
            jax.ShapeDtypeStruct((length // CHUNK, STATE, WIDE), f32),
            jax.ShapeDtypeStruct((length, D), low),
            jax.ShapeDtypeStruct((8, length), f32),
        ],
        scratch_shapes=[pltpu.VMEM((BLOCK + 8, 512), f32), pltpu.VMEM((STATE, WIDE), f32)],
        compiler_params=pltpu.CompilerParams(
            dimension_semantics=("arbitrary",), vmem_limit_bytes=56 * 1024 * 1024
        ),
        name="ssd_forward",
    )(both, w, w_out, rows, conv, heads, skip)


def ssd_backward(place, both, w, proj, rows, conv, heads, skip, y, gated, u, kept):
    length = proj.shape[0]
    steps = length // BLOCK
    back = lambda i: steps - 1 - i
    whole = lambda shape: pl.BlockSpec(shape, lambda i: (0,) * len(shape))
    here = lambda width: pl.BlockSpec((BLOCK, width), lambda i: (back(i), 0))
    return pl.pallas_call(
        backward_kernel,
        grid=(steps,),
        in_specs=[
            pl.BlockSpec(memory_space=pltpu.SMEM),
            here(PAD),
            pl.BlockSpec((16, PAD), lambda i: (jnp.maximum(back(i) * (BLOCK // 16) - 1, 0), 0)),
            whole((D, PAD)),
            pl.BlockSpec((BLOCK, D), lambda i: (back(i), 1)),
            pl.BlockSpec((GROUP, 8, CHUNK), lambda i: (back(i), 0, 0)),
            whole((8, 512)),
            whole((2, 8 * GROUP, CHUNK)),
            whole((1, WIDE)),
            here(WIDE),
            here(WIDE),
            here(WIDE),
            pl.BlockSpec((GROUP, STATE, WIDE), lambda i: (back(i), 0, 0)),
        ],
        out_specs=[
            here(PAD),
            whole((4, 4, 64, D)),
            whole((4, 4, 64, D)),
            whole((WIDE, D)),
            whole((16, 512)),
        ],
        out_shape=[
            jax.ShapeDtypeStruct((length, PAD), low),
            jax.ShapeDtypeStruct((4, 4, 64, D), low),
            jax.ShapeDtypeStruct((4, 4, 64, D), low),
            jax.ShapeDtypeStruct((WIDE, D), f32),
            jax.ShapeDtypeStruct((16, 512), f32),
        ],
        scratch_shapes=[
            pltpu.VMEM((BLOCK + 8, 512), f32),
            pltpu.VMEM((BLOCK + 8, 512), f32),
            pltpu.VMEM((STATE, WIDE), f32),
            pltpu.VMEM((CONV + 1, 8, 512), f32),
            pltpu.VMEM((2, 8, CHUNK), f32),
            pltpu.VMEM((8, WIDE), f32),
        ],
        compiler_params=pltpu.CompilerParams(
            dimension_semantics=("arbitrary",), vmem_limit_bytes=56 * 1024 * 1024
        ),
        name="ssd_backward",
    )(place, proj, proj, w, both, rows, conv, heads, skip, y, gated, u, kept)


epsilon = 1e-05
BOTH = ("dp", "seq")


def columns_of(a, small):
    rows = a.shape[0]
    z = a[:, :INNER].reshape(rows, 16, WIDE)
    x = a[:, INNER : 2 * INNER].reshape(rows, 16, WIDE)
    bc = jnp.broadcast_to(a[:, None, 2 * INNER : 2 * INNER + 256], (rows, 16, 256))
    dt = a[:, 2 * INNER + 256 :].reshape(rows, 16, OWN)
    blank = lambda n: jnp.zeros((rows, 16, n), a.dtype)
    small = jnp.broadcast_to(small[:, None], (rows, 16, 22))
    return jnp.concatenate([z, dt, blank(61), x, small, blank(42), bc], axis=2).transpose(1, 0, 2)


def padded(a):
    return jnp.concatenate(
        [a[:, :WIDE], jnp.zeros((a.shape[0], 64), a.dtype), a[:, WIDE:]], axis=1
    )


def along_x(a, k):
    return lax.ppermute(a, "seq", [(s, (s // 4) * 4 + (s % 4 + k) % 4) for s in range(16)])


def along_y(a, k):
    return lax.ppermute(a, "seq", [(s, ((s // 4 + k) % 4) * 4 + s % 4) for s in range(16)])


def along_z(a, k):
    return lax.ppermute(a, "dp", [(d, ((d // 2 + k) % 4) * 2 + d % 2) for d in range(8)])


def other_core(a):
    return lax.ppermute(a, "dp", [(d, d ^ 1) for d in range(8)])


def put(buf, piece, *at):
    return lax.dynamic_update_slice(buf, piece, tuple(at) + (0,) * (buf.ndim - len(at)))


def take(a, i):
    return lax.dynamic_index_in_dim(a, i % a.shape[0], 0, False)


def added(a, b):
    return (a.astype(f32) + b.astype(f32)).astype(low)


def scattered_sum(top, bottom):
    me = lax.axis_index("seq")
    x, y = me % 4, me // 4
    total = lambda own, others: sum([o.astype(f32) for o in others], own.astype(f32))
    top = total(top[0], [along_y(top[k], k) for k in (2, 1, 3)]).astype(low)
    bottom = total(bottom[0], [along_x(bottom[k], k) for k in (2, 1, 3)]).astype(low)
    own_top = total(take(top, x), [along_x(take(top, x + k), k) for k in (2, 1, 3)])
    own_bottom = total(take(bottom, y), [along_y(take(bottom, y + k), k) for k in (2, 1, 3)])
    return jnp.concatenate([own_top, own_bottom], axis=0)


def gathered_z(a):
    d = lax.axis_index("dp")
    z, core = d // 2, d % 2
    h = a.shape[0] // 2
    first, last = a[:h], a[h:]
    up_first = along_z(first, 1)
    down_last = along_z(last, 3)
    up_last = along_z(last, 1)
    down_first = along_z(first, 3)
    far_first = along_z(up_first, 1)
    far_last = along_z(down_last, 3)
    mine = put(jnp.zeros((4, 2, h, a.shape[1]), a.dtype), a.reshape(1, 2, h, -1), z)
    for k, p, q in ((3, up_first, up_last), (1, down_first, down_last), (2, far_first, far_last)):
        mine = put(mine, p[None, None], (z + k) % 4, 0)
        mine = put(mine, q[None, None], (z + k) % 4, 1)
    mine = mine.reshape(4, 1, 2 * h, -1)
    other = other_core(mine)
    first = core == 0
    pair = (jnp.where(first, mine, other), jnp.where(first, other, mine))
    return jnp.concatenate(pair, axis=1).reshape(8, 2 * h, -1)


def seq_sum(a):
    a = a + along_x(a, 1) + along_x(a, 3) + along_x(a, 2)
    return a + along_y(a, 1) + along_y(a, 3) + along_y(a, 2)


def block_order(back):
    pairs = [(f, (f % 8) * 16 + f // 8) for f in range(128)]
    return [(b, a) for a, b in pairs] if back else pairs


def local(
    hidden,
    segments,
    pre_gain,
    w_in,
    conv_weight,
    conv_bias,
    dt_bias,
    a_log,
    d_skip,
    gate_gain,
    w_out,
    grad_out,
):
    me = lax.axis_index("seq")
    row = lax.axis_index("dp")
    tokens = hidden[0].astype(f32)
    r0 = lax.rsqrt(jnp.mean(tokens * tokens, axis=-1, keepdims=True) + epsilon)
    hn = (tokens * r0).astype(low)
    both = jnp.concatenate([hn, grad_out[0]], axis=1)
    both = lax.all_gather(both, "seq", axis=0, tiled=True)

    gain_in = pre_gain.astype(f32)[:, None]
    gain_out = gate_gain.astype(f32)[:, None]
    w_in_wide = w_in.astype(f32)
    w_out_wide = w_out.astype(f32)
    small = jnp.concatenate([conv_weight.reshape(-1), conv_bias, segments[0].astype(low)])
    small = jnp.pad(small, (0, 264 - small.shape[0])).reshape(12, 22)
    parts = columns_of((w_in_wide * gain_in).astype(low), small).reshape(16 * 12, PAD)
    parts = lax.all_to_all(parts, "seq", 0, 0, tiled=True)
    segment = parts[:, 448:470].reshape(16, 264)[:, 130:258].astype(f32).reshape(1, 2048)
    before = jnp.concatenate([jnp.full((1, 1), -1.0, f32), segment[:, :-1]], axis=1)
    blocks = lax.ppermute((w_out_wide * gain_out).astype(low), BOTH, block_order(False))
    weights = gathered_z(jnp.concatenate([parts, blocks.reshape(48, PAD)], axis=0))
    w_own = weights[:, :192].reshape(D, PAD)
    w_out_own = weights[:, 192:].reshape(WIDE, D)
    conv_all = weights[:, :192, 448:470].reshape(128, 264)[:, :130].astype(f32)
    conv_all = conv_all.reshape(128, 5, 26).transpose(1, 0, 2).reshape(5, CONV_CH)
    conv = jnp.concatenate(
        [lax.dynamic_slice_in_dim(conv_all, me * WIDE, WIDE, 1), conv_all[:, INNER:]], axis=1
    )
    conv = jnp.concatenate([padded(conv), jnp.zeros((3, 512), f32)], axis=0)
    own = lambda a: lax.dynamic_slice_in_dim(a, me * OWN, OWN, 0)
    tall = lambda a: jnp.broadcast_to(
        jnp.tile(jnp.pad(own(a), (0, 8 - OWN)), GROUP)[:, None], (8 * GROUP, CHUNK)
    )
    heads = jnp.stack([tall(dt_bias), tall(a_log)])
    skip = jnp.repeat(own(d_skip), 64)[None]
    by_chunk = lambda rows: jnp.concatenate(
        rows + [jnp.zeros((8 - len(rows), 2048), f32)], axis=0
    ).reshape(8, 16, CHUNK).transpose(1, 0, 2)

    proj, y, gated, u, kept, partial_out, sums = ssd_forward(
        both, w_own, w_out_own, by_chunk([segment, before]), conv, heads, skip
    )
    total = lax.psum_scatter(partial_out, "seq", scatter_dimension=0, tiled=True)
    sums = seq_sum(sums[:2].reshape(32, 128)).reshape(2, 2048)
    r = lax.rsqrt(sums[0:1] / INNER + epsilon)
    c = r * r * r * (sums[1:2] / INNER)

    place = jnp.stack([me % 4, me // 4])
    d_proj, top, bottom, grad_out_w, small = ssd_backward(
        place, both, w_own, proj, by_chunk([segment, before, r, c]), conv, heads, skip, y, gated, u, kept
    )
    v = scattered_sum(top, bottom)
    grad_in = lax.dot_general(
        both[:, :D], d_proj, (((0,), (0,)), ((), ())), preferred_element_type=f32
    )
    grads = jnp.concatenate(
        [grad_in.reshape(8, 192, PAD), grad_out_w.reshape(8, 48, PAD)], axis=1
    ).astype(low)
    grads, total = lax.optimization_barrier((grads, total))
    grads = lax.psum_scatter(grads.reshape(8 * 240, PAD), "dp", scatter_dimension=0, tiled=True)
    conv_flat = jnp.zeros((5, CONV_CH), f32)
    conv_flat = lax.dynamic_update_slice(conv_flat, small[:5, 256:], (0, INNER))
    conv_flat = lax.dynamic_update_slice(conv_flat, small[:5, :WIDE], (0, me * WIDE))
    conv_flat = conv_flat.reshape(5, 128, 26).transpose(1, 0, 2).reshape(128, 130)
    head_own = jnp.concatenate(
        [small[8:11, 0], small[8:11, 1], small[5, :WIDE].reshape(OWN, 64).sum(axis=1)]
    )
    small = jnp.concatenate([conv_flat, jnp.broadcast_to(head_own[None], (128, 9))], axis=1)
    small = lax.all_to_all(small, BOTH, 0, 0, tiled=True)
    conv_sum = jnp.sum(small[:, :130], axis=0).reshape(5, 26)
    head_sum = jnp.sum(small[:, 130:].reshape(8, 16, 3, OWN), axis=0)
    head_sum = head_sum.transpose(1, 0, 2).reshape(3, HEADS)
    g_parts = lax.all_to_all(grads[:192], "seq", 0, 0, tiled=True).reshape(16, 12, PAD)
    g_out = lax.ppermute(grads[192:].reshape(24, D), BOTH, block_order(True)).astype(f32)
    g_parts = g_parts.astype(f32).transpose(1, 0, 2)
    g_in = jnp.concatenate(
        [
            g_parts[:, :, :WIDE].reshape(12, INNER),
            g_parts[:, :, 256 : 256 + WIDE].reshape(12, INNER),
            jnp.sum(g_parts[:, :, 512:], axis=1),
            g_parts[:, :, WIDE : WIDE + OWN].reshape(12, HEADS),
        ],
        axis=1,
    )
    grad_w_in = gain_in * g_in
    grad_pre_gain = jnp.sum(w_in_wide * g_in, axis=1)
    grad_w_out = gain_out * g_out
    grad_gate_gain = jnp.sum(w_out_wide * g_out, axis=1)
    r_own = lax.dynamic_slice_in_dim(r[0], me * 128, 128, 0)
    block_out = (r_own[:, None] * total.astype(f32) + tokens).astype(low)
    mean = jnp.mean(v * tokens, axis=-1, keepdims=True)
    grad_hidden = (
        grad_out[0].astype(f32) + r0 * v - tokens * (r0 * r0 * r0 * mean)
    ).astype(low)
    return (
        block_out[None],
        grad_hidden[None],
        grad_pre_gain,
        grad_w_in,
        conv_sum[:CONV],
        conv_sum[CONV],
        head_sum[0],
        head_sum[1],
        head_sum[2],
        grad_gate_gain,
        grad_w_out,
    )


def solution(mesh):
    placed = (
        P("dp", "seq", None),
        P("dp", "seq"),
        P(BOTH),
        P(BOTH, None),
        P(None, BOTH),
        P(BOTH),
        P(),
        P(),
        P(),
        P(BOTH),
        P(BOTH, None),
        P("dp", "seq", None),
    )
    return jax.shard_map(
        local,
        mesh=mesh,
        in_specs=placed,
        out_specs=(
            P("dp", "seq", None),
            P("dp", "seq", None),
            P(BOTH),
            P(BOTH, None),
            P(None, BOTH),
            P(BOTH),
            P(),
            P(),
            P(),
            P(BOTH),
            P(BOTH, None),
        ),
        check_vma=False,
    )
```

```python
import jax
import jax.numpy as jnp
from jax import lax
from jax.experimental import pallas as pl
from jax.experimental.pallas import tpu as pltpu
from jax.sharding import PartitionSpec as P

D = 1536
INNER = 3072
STATE = 128
CONV = 4
HEADS = 48
CONV_CH = 3328
CHUNK = 128
GROUP = 4
BLOCK = CHUNK * GROUP
OWN = 3
WIDE = 192
PAD = 768
low = jnp.bfloat16
f32 = jnp.float32


def mm(a, b, dims=((1,), (0,))):
    return lax.dot_general(a, b, (dims, ((), ())), preferred_element_type=f32)


NT = ((1,), (1,))
TN = ((0,), (0,))


def per_head(parts):
    lane = lax.broadcasted_iota(jnp.int32, (1, WIDE), 1)
    return jnp.where(lane < 64, parts[0], jnp.where(lane < 128, parts[1], parts[2]))


def stacked(a):
    lane = lax.broadcasted_iota(jnp.int32, a.shape, 1)
    zero = jnp.zeros_like(a)
    return jnp.concatenate(
        [jnp.where((lane >= 64 * h) & (lane < 64 * h + 64), a, zero) for h in range(OWN)], axis=0
    )


def running(a, back):
    lane = lax.broadcasted_iota(jnp.int32, a.shape, 1)
    step = 1
    while step < CHUNK:
        if back:
            a = a + jnp.where(lane < CHUNK - step, pltpu.roll(a, CHUNK - step, 1), 0.0)
        else:
            a = a + jnp.where(lane >= step, pltpu.roll(a, step, 1), 0.0)
        step *= 2
    return a


def part(a, j):
    return a[CHUNK * j : CHUNK * (j + 1)]


def eight(a, j):
    return a[8 * j : 8 * (j + 1)]


def block_terms(zdt, rows_ref, head_ref):
    raw = jnp.concatenate([part(zdt, j)[:, 128:256].T[64:72] for j in range(GROUP)], axis=0)
    wide = lambda row: jnp.concatenate(
        [jnp.broadcast_to(rows_ref[j, row : row + 1, :], (8, CHUNK)) for j in range(GROUP)], axis=0
    )
    v = raw + head_ref[0]
    ea = jnp.exp(head_ref[1])
    step = jnp.maximum(v, 0.0) + jnp.log1p(jnp.exp(-jnp.abs(v)))
    ld = -step * ea
    cum = running(ld, False)
    total = cum[:, CHUNK - 1 : CHUNK]
    seg = wide(0)
    before = wide(1)[:, 0:1]
    last = seg[:, CHUNK - 1 : CHUNK]
    entry = jnp.exp(cum) * (seg == before).astype(f32)
    to_end = jnp.exp(total - cum) * (seg == last).astype(f32)
    whole = jnp.exp(total) * (last == before).astype(f32)
    leaving = to_end * step
    cols = []
    for j in range(GROUP):
        pack = [eight(cum, j), eight(entry, j), eight(leaving, j), rows_ref[j]]
        pack = jnp.concatenate(pack + [jnp.zeros((CHUNK - 32, CHUNK), f32)], axis=0)
        cols.append(pack.T)
    return v, ea, step, ld, cum, to_end, whole, cols


def barred(cols, seg):
    t = lax.broadcasted_iota(jnp.int32, (CHUNK, CHUNK), 0)
    s = lax.broadcasted_iota(jnp.int32, (CHUNK, CHUNK), 1)
    return jnp.where((t >= s) & (cols[:, 24:25] == seg), 0.0, -1e30)


def convolved(ext_ref, conv_ref):
    pre = conv_ref[CONV : CONV + 1, :]
    for k in range(CONV):
        pre = pre + conv_ref[k : k + 1, :] * ext_ref[pl.ds(5 + k, BLOCK), :]
    return pre


def forward_kernel(
    both_ref,
    w_ref,
    out_ref,
    rows_ref,
    conv_ref,
    head_ref,
    skip_ref,
    proj_ref,
    y_ref,
    gated_ref,
    u_ref,
    kept_ref,
    total_ref,
    sums_ref,
    ext_ref,
    state_ref,
):
    first = pl.program_id(0) == 0

    @pl.when(first)
    def _():
        ext_ref[0:8, :] = jnp.zeros((8, 512), f32)
        state_ref[...] = jnp.zeros_like(state_ref)

    @pl.when(jnp.logical_not(first))
    def _():
        ext_ref[0:8, :] = ext_ref[BLOCK : BLOCK + 8, :]

    proj_ref[...] = mm(both_ref[:, 0:D], w_ref[...]).astype(low)
    u_ref[...] = mm(both_ref[:, D : 2 * D], out_ref[...], NT)
    zdt = proj_ref[:, 0:256].astype(f32)
    ext_ref[8 : BLOCK + 8, :] = proj_ref[:, 256:PAD].astype(f32)
    pre = convolved(ext_ref, conv_ref)
    act = pre * jax.nn.sigmoid(pre)
    x = act[:, :WIDE]
    x_low = x.astype(low)
    b_low = act[:, 256:384].astype(low)
    c_low = act[:, 384:512].astype(low)
    v, ea, step, ld, cum, to_end, whole, cols = block_terms(zdt, rows_ref, head_ref)
    inner, local, entries, wholes = [], [], [], []
    for j in range(GROUP):
        col = cols[j]
        bar = barred(col, rows_ref[j, 0:1, :])
        scores = mm(part(c_low, j), part(b_low, j), NT)
        mixing = []
        for h in range(OWN):
            i = 8 * j + h
            decay = jnp.exp(col[:, h : h + 1] - cum[i : i + 1] + bar)
            mixing.append((scores * decay * step[i : i + 1]).astype(low))
        inner.append(mm(jnp.concatenate(mixing, axis=1), stacked(part(x_low, j))))
        leaving = per_head([col[:, 16 + h : 17 + h] for h in range(OWN)])
        local.append(mm(part(b_low, j), (leaving * part(x, j)).astype(low), TN))
        entries.append(per_head([col[:, 8 + h : 9 + h] for h in range(OWN)]))
        wholes.append(per_head([whole[8 * j + h : 8 * j + h + 1] for h in range(OWN)]))
    state = state_ref[...]
    ys = []
    for j in range(GROUP):
        kept_ref[j] = state
        ys.append(inner[j] + entries[j] * mm(part(c_low, j), state.astype(low)))
        state = wholes[j] * state + local[j]
    state_ref[...] = state
    y = jnp.concatenate(ys, axis=0) + skip_ref[...] * x
    z = zdt[:, :WIDE]
    gated = y * z * jax.nn.sigmoid(z)
    gated_low = gated.astype(low)
    y_ref[...] = y
    gated_ref[...] = gated_low
    total_ref[...] = mm(gated_low, out_ref[...]).astype(low)
    ones = jnp.ones((8, WIDE), low)
    squares = mm(ones, (gated * gated).astype(low), NT)
    products = mm(ones, (gated * u_ref[...]).astype(low), NT)
    row = lax.broadcasted_iota(jnp.int32, (8, BLOCK), 0)
    sums_ref[...] = jnp.where(row == 0, squares, products)


def backward_kernel(
    place_ref,
    proj_ref,
    before_ref,
    w_ref,
    both_ref,
    rows_ref,
    conv_ref,
    head_ref,
    skip_ref,
    y_ref,
    gated_ref,
    u_ref,
    kept_ref,
    top_0,
    top_1,
    top_2,
    top_3,
    bottom_0,
    bottom_1,
    bottom_2,
    bottom_3,
    grads_ref,
    ext_ref,
    later_ref,
    state_ref,
    conv_grad_ref,
    head_grad_ref,
    skip_grad_ref,
    d_proj_ref,
    given_ref,
    total_ref,
    sums_ref,
):
    step_id = pl.program_id(0)
    count = pl.num_programs(0)

    @pl.when(step_id == 0)
    def _():
        later_ref[BLOCK : BLOCK + 8, :] = jnp.zeros((8, 512), f32)
        state_ref[...] = jnp.zeros_like(state_ref)
        conv_grad_ref[...] = jnp.zeros_like(conv_grad_ref)
        head_grad_ref[...] = jnp.zeros_like(head_grad_ref)
        skip_grad_ref[...] = jnp.zeros_like(skip_grad_ref)
        total_ref[...] = jnp.zeros_like(total_ref)

    @pl.when(step_id > 0)
    def _():
        later_ref[BLOCK : BLOCK + 8, :] = later_ref[0:8, :]

    ahead = before_ref[8:16, 256:PAD].astype(f32)
    ext_ref[0:8, :] = jnp.where(step_id == count - 1, 0.0, ahead)
    conv_in = proj_ref[:, 256:PAD].astype(f32)
    ext_ref[8 : BLOCK + 8, :] = conv_in
    zdt = proj_ref[:, 0:256].astype(f32)
    pre = convolved(ext_ref, conv_ref)
    sig = jax.nn.sigmoid(pre)
    act = pre * sig
    slope = sig * (1.0 + pre * (1.0 - sig))
    x = act[:, :WIDE]
    x_low = x.astype(low)
    b_low = act[:, 256:384].astype(low)
    c_low = act[:, 384:512].astype(low)
    v, ea, step, ld, cum, to_end, whole, cols = block_terms(zdt, rows_ref, head_ref)

    z = zdt[:, :WIDE]
    z_sig = jax.nn.sigmoid(z)
    z_act = z * z_sig
    y = y_ref[...]
    r_col = jnp.concatenate([c[:, 26:27] for c in cols], axis=0)
    c_col = jnp.concatenate([c[:, 27:28] for c in cols], axis=0)
    d_gated = r_col * u_ref[...] - c_col * (y * z_act)
    dy = d_gated * z_act
    dz = d_gated * y * (z_sig * (1.0 + z * (1.0 - z_sig)))
    dy_low = dy.astype(low)
    normed = (gated_ref[...].astype(f32) * r_col).astype(low)
    out_grad = mm(normed, both_ref[:, D : 2 * D], TN)
    for d in range(8):
        total_ref[d, 192:216] += out_grad[24 * d : 24 * d + 24, 0:PAD]
        total_ref[d, 216:240] += out_grad[24 * d : 24 * d + 24, PAD:D]

    t = lax.broadcasted_iota(jnp.int32, (CHUNK, CHUNK), 0)
    s = lax.broadcasted_iota(jnp.int32, (CHUNK, CHUNK), 1)
    earlier = (t < s).astype(low)
    blank = jnp.zeros((8 - OWN, CHUNK), f32)
    row_head = lax.broadcasted_iota(jnp.int32, (8, WIDE), 0)
    lane = lax.broadcasted_iota(jnp.int32, (8, WIDE), 1)
    by_head = ((lane >= 64 * row_head) & (lane < 64 * row_head + 64)).astype(low)

    dx_in, d_scores_all, d_steps_all, inside_all = [], [], [], []
    entries, leavings, wholes, to_state, dy_entries = [], [], [], [], []
    for j in range(GROUP):
        col = cols[j]
        bar = barred(col, rows_ref[j, 0:1, :])
        scores = mm(part(c_low, j), part(b_low, j), NT)
        d_mixing = mm(part(dy_low, j), stacked(part(x_low, j)), NT)
        d_scores = jnp.zeros((CHUNK, CHUNK), f32)
        mixings, flows, d_steps = [], [], []
        for h in range(OWN):
            i = 8 * j + h
            decay = jnp.exp(col[:, h : h + 1] - cum[i : i + 1] + bar)
            stepped = decay * step[i : i + 1]
            mixing = scores * stepped
            mixings.append(mixing.astype(low))
            d_mix = d_mixing[:, CHUNK * h : CHUNK * h + CHUNK]
            d_scores = d_scores + d_mix * stepped
            flows.append((d_mix * mixing).astype(low))
            d_steps.append(jnp.sum(d_mix * scores * decay, axis=0, keepdims=True))
        reach = mm(jnp.concatenate(flows, axis=0), earlier)
        inside = [
            jnp.sum(jnp.where(t >= s, part(reach, h), 0.0), axis=0, keepdims=True)
            for h in range(OWN)
        ]
        d_scores_all.append(d_scores.astype(low))
        d_steps_all += d_steps + [blank]
        inside_all += inside + [blank]
        dx_in.append(mm(jnp.concatenate(mixings, axis=0), stacked(part(dy_low, j)), TN))
        entry = per_head([col[:, 8 + h : 9 + h] for h in range(OWN)])
        dy_entry = entry * part(dy, j)
        dy_entries.append(dy_entry)
        to_state.append(mm(part(c_low, j), dy_entry.astype(low), TN))
        leavings.append(per_head([col[:, 16 + h : 17 + h] for h in range(OWN)]))
        wholes.append(per_head([whole[8 * j + h : 8 * j + h + 1] for h in range(OWN)]))

    laters = [None] * GROUP
    later = state_ref[...]
    for j in reversed(range(GROUP)):
        laters[j] = later
        later = wholes[j] * later + to_state[j]
    state_ref[...] = later

    xv, row_state, overlap, dxs, dbs, dcs = [], [], [], [], [], []
    for j in range(GROUP):
        bj, cj, xj = part(b_low, j), part(c_low, j), part(x, j)
        state_low = kept_ref[j].astype(low)
        later_low = laters[j].astype(low)
        from_later = mm(bj, later_low)
        dxs.append(dx_in[j] + leavings[j] * from_later)
        x_leaving = (leavings[j] * xj).astype(low)
        d_scores = d_scores_all[j]
        dcs.append(mm(d_scores, bj) + mm(dy_entries[j].astype(low), state_low, NT))
        dbs.append(mm(d_scores, cj, TN) + mm(x_leaving, later_low, NT))
        xv.append(mm(by_head, (xj * from_later).astype(low), NT))
        row_state.append(mm(by_head, (dy_entries[j] * mm(cj, state_low)).astype(low), NT))
        both = mm(by_head, (laters[j] * kept_ref[j]).astype(low), NT)
        overlap.append(jnp.sum(both, axis=1, keepdims=True))
    stack = lambda a: jnp.concatenate(a, axis=0)
    ended = to_end * stack(xv)
    col_state = ended * step
    d_step = stack(d_steps_all) + ended
    d_ld = (
        stack(inside_all)
        + running(stack(row_state), True)
        + (running(col_state, False) - col_state)
        + whole * stack(overlap)
    )
    d_dt = (d_step - d_ld * ea) * jax.nn.sigmoid(v)
    head_grad_ref[0] += sum([eight(d_dt, j) for j in range(GROUP)])
    head_grad_ref[1] += sum([eight(d_ld * ld, j) for j in range(GROUP)])
    skip_grad_ref[...] += jnp.sum((dy * x).reshape(BLOCK // 8, 8, WIDE), axis=0)

    dx = stack(dxs) + skip_ref[...] * dy
    later_ref[0:BLOCK, 0:WIDE] = dx * slope[:, :WIDE]
    later_ref[0:BLOCK, WIDE:256] = jnp.zeros((BLOCK, 256 - WIDE), f32)
    later_ref[0:BLOCK, 256:384] = stack(dbs) * slope[:, 256:384]
    later_ref[0:BLOCK, 384:512] = stack(dcs) * slope[:, 384:512]
    d_conv_in = jnp.zeros((BLOCK, 512), f32)
    for k in range(CONV):
        moved = later_ref[pl.ds(CONV - 1 - k, BLOCK), :]
        d_conv_in = d_conv_in + conv_ref[k : k + 1, :] * moved
        conv_grad_ref[k] += jnp.sum((moved * conv_in).reshape(BLOCK // 8, 8, 512), axis=0)
        if k == CONV - 1:
            conv_grad_ref[CONV] += jnp.sum(moved.reshape(BLOCK // 8, 8, 512), axis=0)

    turned = []
    for j in range(GROUP):
        tall = [jnp.zeros((64, CHUNK), f32), eight(d_dt, j), jnp.zeros((56, CHUNK), f32)]
        turned.append(jnp.concatenate(tall, axis=0).T)
    d_proj_ref[:, 0:128] = dz[:, 0:128].astype(low)
    d_proj_ref[:, 128:256] = jnp.concatenate(
        [dz[:, 128:WIDE], stack(turned)[:, 64:128]], axis=1
    ).astype(low)
    d_proj_ref[:, 256:PAD] = d_conv_in.astype(low)

    in_grad = mm(both_ref[:, 0:D], d_proj_ref[...], TN)
    for d in range(8):
        total_ref[d, 0:192] += in_grad[192 * d : 192 * d + 192]

    given_ref[...] = mm(d_proj_ref[...], w_ref[...], NT).astype(low)
    row = count - 1 - step_id
    up = lax.rem(row - place_ref[1] + 4, 4)
    for k, ref in enumerate((top_0, top_1, top_2, top_3)):

        @pl.when(up == k)
        def _():
            for j in range(GROUP):
                ref[j] = given_ref[CHUNK * j : CHUNK * j + 64, :]

    for k, ref in enumerate((bottom_0, bottom_1, bottom_2, bottom_3)):
        for j in range(GROUP):

            @pl.when(lax.rem(j - place_ref[0] + 4, 4) == k)
            def _():
                ref[row] = given_ref[CHUNK * j + 64 : CHUNK * (j + 1), :]

    @pl.when(step_id == count - 1)
    def _():
        place = lax.broadcasted_iota(jnp.int32, (8, 256), 1)
        bias = jnp.sum(head_grad_ref[0], axis=1, keepdims=True)
        rate = jnp.sum(head_grad_ref[1], axis=1, keepdims=True)
        sums_ref[:, 512:PAD] = jnp.where(place == 0, bias, jnp.where(place == 1, rate, 0.0))
        for k in range(CONV + 1):
            sums_ref[k : k + 1, 0:512] = jnp.sum(conv_grad_ref[k], axis=0, keepdims=True)
        sums_ref[5:8, 0:512] = jnp.zeros((3, 512), f32)
        sums_ref[5:6, 0:WIDE] = jnp.sum(skip_grad_ref[...], axis=0, keepdims=True)
        sums = sums_ref[...]
        high = sums.astype(low).astype(f32)
        tail = jnp.concatenate([high, sums - high], axis=0).astype(low)
        for d in range(8):
            grads_ref[d, 0:240] = total_ref[d].astype(low)
            grads_ref[d, 240:256] = tail


def ssd_forward(both, w, w_out, rows, conv, heads, skip):
    length = both.shape[0]
    steps = length // BLOCK
    whole = lambda shape: pl.BlockSpec(shape, lambda i: (0,) * len(shape))
    here = lambda width: pl.BlockSpec((BLOCK, width), lambda i: (i, 0))
    return pl.pallas_call(
        forward_kernel,
        grid=(steps,),
        in_specs=[
            here(2 * D),
            whole((D, PAD)),
            whole((WIDE, D)),
            pl.BlockSpec((GROUP, 8, CHUNK), lambda i: (i, 0, 0)),
            whole((8, 512)),
            whole((2, 8 * GROUP, CHUNK)),
            whole((1, WIDE)),
        ],
        out_specs=[
            here(PAD),
            here(WIDE),
            here(WIDE),
            here(WIDE),
            pl.BlockSpec((GROUP, STATE, WIDE), lambda i: (i, 0, 0)),
            here(D),
            pl.BlockSpec((8, BLOCK), lambda i: (0, i)),
        ],
        out_shape=[
            jax.ShapeDtypeStruct((length, PAD), low),
            jax.ShapeDtypeStruct((length, WIDE), f32),
            jax.ShapeDtypeStruct((length, WIDE), low),
            jax.ShapeDtypeStruct((length, WIDE), f32),
            jax.ShapeDtypeStruct((length // CHUNK, STATE, WIDE), f32),
            jax.ShapeDtypeStruct((length, D), low),
            jax.ShapeDtypeStruct((8, length), f32),
        ],
        scratch_shapes=[pltpu.VMEM((BLOCK + 8, 512), f32), pltpu.VMEM((STATE, WIDE), f32)],
        compiler_params=pltpu.CompilerParams(
            dimension_semantics=("arbitrary",), vmem_limit_bytes=56 * 1024 * 1024
        ),
        name="ssd_forward",
    )(both, w, w_out, rows, conv, heads, skip)


def ssd_backward(place, both, w, proj, rows, conv, heads, skip, y, gated, u, kept):
    length = proj.shape[0]
    steps = length // BLOCK
    back = lambda i: steps - 1 - i
    whole = lambda shape: pl.BlockSpec(shape, lambda i: (0,) * len(shape))
    here = lambda width: pl.BlockSpec((BLOCK, width), lambda i: (back(i), 0))
    return pl.pallas_call(
        backward_kernel,
        grid=(steps,),
        in_specs=[
            pl.BlockSpec(memory_space=pltpu.SMEM),
            here(PAD),
            pl.BlockSpec((16, PAD), lambda i: (jnp.maximum(back(i) * (BLOCK // 16) - 1, 0), 0)),
            whole((D, PAD)),
            here(2 * D),
            pl.BlockSpec((GROUP, 8, CHUNK), lambda i: (back(i), 0, 0)),
            whole((8, 512)),
            whole((2, 8 * GROUP, CHUNK)),
            whole((1, WIDE)),
            here(WIDE),
            here(WIDE),
            here(WIDE),
            pl.BlockSpec((GROUP, STATE, WIDE), lambda i: (back(i), 0, 0)),
        ],
        out_specs=[
            *[whole((4, 64, D)) for _ in range(8)],
            whole((8, 256, PAD)),
        ],
        out_shape=[
            *[jax.ShapeDtypeStruct((4, 64, D), low) for _ in range(8)],
            jax.ShapeDtypeStruct((8, 256, PAD), low),
        ],
        scratch_shapes=[
            pltpu.VMEM((BLOCK + 8, 512), f32),
            pltpu.VMEM((BLOCK + 8, 512), f32),
            pltpu.VMEM((STATE, WIDE), f32),
            pltpu.VMEM((CONV + 1, 8, 512), f32),
            pltpu.VMEM((2, 8, CHUNK), f32),
            pltpu.VMEM((8, WIDE), f32),
            pltpu.VMEM((BLOCK, PAD), low),
            pltpu.VMEM((BLOCK, D), low),
            pltpu.VMEM((8, 240, PAD), f32),
            pltpu.VMEM((8, PAD), f32),
        ],
        compiler_params=pltpu.CompilerParams(
            dimension_semantics=("arbitrary",), vmem_limit_bytes=56 * 1024 * 1024
        ),
        name="ssd_backward",
    )(place, proj, proj, w, both, rows, conv, heads, skip, y, gated, u, kept)


epsilon = 1e-05
BOTH = ("dp", "seq")


def columns_of(a, small):
    rows = a.shape[0]
    z = a[:, :INNER].reshape(rows, 16, WIDE)
    x = a[:, INNER : 2 * INNER].reshape(rows, 16, WIDE)
    bc = jnp.broadcast_to(a[:, None, 2 * INNER : 2 * INNER + 256], (rows, 16, 256))
    dt = a[:, 2 * INNER + 256 :].reshape(rows, 16, OWN)
    blank = lambda n: jnp.zeros((rows, 16, n), a.dtype)
    small = jnp.broadcast_to(small[:, None], (rows, 16, 22))
    return jnp.concatenate([z, dt, blank(61), x, small, blank(42), bc], axis=2).transpose(1, 0, 2)


def padded(a):
    return jnp.concatenate(
        [a[:, :WIDE], jnp.zeros((a.shape[0], 64), a.dtype), a[:, WIDE:]], axis=1
    )


def along_x(a, k):
    return lax.ppermute(a, "seq", [(s, (s // 4) * 4 + (s % 4 + k) % 4) for s in range(16)])


def along_y(a, k):
    return lax.ppermute(a, "seq", [(s, ((s // 4 + k) % 4) * 4 + s % 4) for s in range(16)])


def along_z(a, k):
    return lax.ppermute(a, "dp", [(d, ((d // 2 + k) % 4) * 2 + d % 2) for d in range(8)])


def other_core(a):
    return lax.ppermute(a, "dp", [(d, d ^ 1) for d in range(8)])


def put(buf, piece, *at):
    return lax.dynamic_update_slice(buf, piece, tuple(at) + (0,) * (buf.ndim - len(at)))


def take(a, i):
    return lax.dynamic_index_in_dim(a, i % a.shape[0], 0, False)


def added(a, b):
    return (a.astype(f32) + b.astype(f32)).astype(low)


def ring_sum(block, along, wait):
    h = block[2].shape[0] // 2
    from_up, from_down = wait((along(block[2][:h], 1), along(block[2][h:], 3)))
    up = jnp.concatenate([added(block[1][:h], from_up), block[1][h:]], axis=0)
    down = jnp.concatenate([block[3][:h], added(block[3][h:], from_down)], axis=0)
    up, down = along(up, 1), along(down, 3)
    return block[0].astype(f32) + up.astype(f32) + down.astype(f32)


def scattered_sum(top, bottom):
    me = lax.axis_index("seq")
    x, y = me % 4, me // 4
    total = lambda own, sent: sum([s.astype(f32) for s in sent], own.astype(f32))
    came = []

    def wait(pieces):
        came.extend(pieces)
        return pieces

    top = ring_sum(top, along_y, wait).astype(low)
    bottom = ring_sum(bottom, along_x, wait).astype(low)
    own_top = total(take(top, x), [along_x(take(top, x + k), k) for k in (2, 1, 3)])
    own_bottom = total(take(bottom, y), [along_y(take(bottom, y + k), k) for k in (2, 1, 3)])
    return jnp.concatenate([own_top, own_bottom], axis=0), came


def gathered_z(a):
    d = lax.axis_index("dp")
    z, core = d // 2, d % 2
    h = a.shape[0] // 2
    first, last = a[:h], a[h:]
    up_first = along_z(first, 1)
    down_last = along_z(last, 3)
    up_last = along_z(last, 1)
    down_first = along_z(first, 3)
    far_first = along_z(up_first, 1)
    far_last = along_z(down_last, 3)
    mine = put(jnp.zeros((4, 2, h, a.shape[1]), a.dtype), a.reshape(1, 2, h, -1), z)
    for k, p, q in ((3, up_first, up_last), (1, down_first, down_last), (2, far_first, far_last)):
        mine = put(mine, p[None, None], (z + k) % 4, 0)
        mine = put(mine, q[None, None], (z + k) % 4, 1)
    mine = mine.reshape(4, 1, 2 * h, -1)
    other = other_core(mine)
    first = core == 0
    pair = (jnp.where(first, mine, other), jnp.where(first, other, mine))
    return jnp.concatenate(pair, axis=1).reshape(8, 2 * h, -1)


def seq_sum(a):
    a = a + along_x(a, 1) + along_x(a, 3) + along_x(a, 2)
    return a + along_y(a, 1) + along_y(a, 3) + along_y(a, 2)


def block_order(back):
    pairs = [(f, (f % 8) * 16 + f // 8) for f in range(128)]
    return [(b, a) for a, b in pairs] if back else pairs


def local(
    hidden,
    segments,
    pre_gain,
    w_in,
    conv_weight,
    conv_bias,
    dt_bias,
    a_log,
    d_skip,
    gate_gain,
    w_out,
    grad_out,
):
    me = lax.axis_index("seq")
    row = lax.axis_index("dp")
    tokens = hidden[0].astype(f32)
    r0 = lax.rsqrt(jnp.mean(tokens * tokens, axis=-1, keepdims=True) + epsilon)
    hn = (tokens * r0).astype(low)
    both = jnp.concatenate([hn, grad_out[0]], axis=1)
    both = lax.all_gather(both, "seq", axis=0, tiled=True)

    gain_in = pre_gain.astype(f32)[:, None]
    gain_out = gate_gain.astype(f32)[:, None]
    w_in_wide = w_in.astype(f32)
    w_out_wide = w_out.astype(f32)
    small = jnp.concatenate([conv_weight.reshape(-1), conv_bias, segments[0].astype(low)])
    small = jnp.pad(small, (0, 264 - small.shape[0])).reshape(12, 22)
    parts = columns_of((w_in_wide * gain_in).astype(low), small).reshape(16 * 12, PAD)
    parts = lax.all_to_all(parts, "seq", 0, 0, tiled=True)
    segment = parts[:, 448:470].reshape(16, 264)[:, 130:258].astype(f32).reshape(1, 2048)
    before = jnp.concatenate([jnp.full((1, 1), -1.0, f32), segment[:, :-1]], axis=1)
    blocks = lax.ppermute((w_out_wide * gain_out).astype(low), BOTH, block_order(False))
    weights = gathered_z(jnp.concatenate([parts, blocks.reshape(48, PAD)], axis=0))
    w_own = weights[:, :192].reshape(D, PAD)
    w_out_own = weights[:, 192:].reshape(WIDE, D)
    conv_all = weights[:, :192, 448:470].reshape(128, 264)[:, :130].astype(f32)
    conv_all = conv_all.reshape(128, 5, 26).transpose(1, 0, 2).reshape(5, CONV_CH)
    conv = jnp.concatenate(
        [lax.dynamic_slice_in_dim(conv_all, me * WIDE, WIDE, 1), conv_all[:, INNER:]], axis=1
    )
    conv = jnp.concatenate([padded(conv), jnp.zeros((3, 512), f32)], axis=0)
    own = lambda a: lax.dynamic_slice_in_dim(a, me * OWN, OWN, 0)
    tall = lambda a: jnp.broadcast_to(
        jnp.tile(jnp.pad(own(a), (0, 8 - OWN)), GROUP)[:, None], (8 * GROUP, CHUNK)
    )
    heads = jnp.stack([tall(dt_bias), tall(a_log)])
    skip = jnp.repeat(own(d_skip), 64)[None]
    by_chunk = lambda rows: jnp.concatenate(
        rows + [jnp.zeros((8 - len(rows), 2048), f32)], axis=0
    ).reshape(8, 16, CHUNK).transpose(1, 0, 2)

    proj, y, gated, u, kept, partial_out, sums = ssd_forward(
        both, w_own, w_out_own, by_chunk([segment, before]), conv, heads, skip
    )
    total = lax.psum_scatter(partial_out, "seq", scatter_dimension=0, tiled=True)
    sums = seq_sum(sums[:2].reshape(32, 128)).reshape(2, 2048)
    r = lax.rsqrt(sums[0:1] / INNER + epsilon)
    c = r * r * r * (sums[1:2] / INNER)

    place = jnp.stack([me % 4, me // 4])
    *pieces, grads = ssd_backward(
        place, both, w_own, proj, by_chunk([segment, before, r, c]), conv, heads, skip, y, gated, u, kept
    )
    v, came = scattered_sum(pieces[:4], pieces[4:])
    grads, total, came = lax.optimization_barrier((grads, total, came))
    grads = lax.psum_scatter(
        grads.reshape(8 * 256, PAD), "dp", scatter_dimension=0, tiled=True
    ).astype(f32)
    small = (grads[240:248] + grads[248:256]).astype(low)
    grads = grads[:240].astype(low)
    g_parts = jnp.concatenate(
        [grads[:192].reshape(16, 12, PAD), jnp.broadcast_to(small[None], (16, 8, PAD))], axis=1
    )
    g_parts = lax.all_to_all(g_parts, "seq", 0, 0)
    small = g_parts[:, 12:].astype(f32)
    g_parts = g_parts[:, :12]
    g_out = lax.ppermute(grads[192:], BOTH, block_order(True)).astype(f32)
    g_out = jnp.concatenate([g_out[:24], g_out[24:]], axis=1)
    conv_sum = jnp.concatenate(
        [
            small[:, : CONV + 1, :WIDE].transpose(1, 0, 2).reshape(CONV + 1, INNER),
            jnp.sum(small[:, : CONV + 1, 256:512], axis=0),
        ],
        axis=1,
    )
    conv_sum = lax.dynamic_slice_in_dim(conv_sum, 26 * (16 * row + me), 26, 1)
    head_sum = (
        small[:, :OWN, 512].reshape(HEADS),
        small[:, :OWN, 513].reshape(HEADS),
        small[:, 5, :WIDE].reshape(HEADS, 64).sum(axis=1),
    )
    g_parts = g_parts.astype(f32).transpose(1, 0, 2)
    g_in = jnp.concatenate(
        [
            g_parts[:, :, :WIDE].reshape(12, INNER),
            g_parts[:, :, 256 : 256 + WIDE].reshape(12, INNER),
            jnp.sum(g_parts[:, :, 512:], axis=1),
            g_parts[:, :, WIDE : WIDE + OWN].reshape(12, HEADS),
        ],
        axis=1,
    )
    grad_w_in = gain_in * g_in
    grad_pre_gain = jnp.sum(w_in_wide * g_in, axis=1)
    grad_w_out = gain_out * g_out
    grad_gate_gain = jnp.sum(w_out_wide * g_out, axis=1)
    r_own = lax.dynamic_slice_in_dim(r[0], me * 128, 128, 0)
    block_out = (r_own[:, None] * total.astype(f32) + tokens).astype(low)
    mean = jnp.mean(v * tokens, axis=-1, keepdims=True)
    grad_hidden = (
        grad_out[0].astype(f32) + r0 * v - tokens * (r0 * r0 * r0 * mean)
    ).astype(low)
    return (
        block_out[None],
        grad_hidden[None],
        grad_pre_gain,
        grad_w_in,
        conv_sum[:CONV],
        conv_sum[CONV],
        head_sum[0],
        head_sum[1],
        head_sum[2],
        grad_gate_gain,
        grad_w_out,
    )


def solution(mesh):
    placed = (
        P("dp", "seq", None),
        P("dp", "seq"),
        P(BOTH),
        P(BOTH, None),
        P(None, BOTH),
        P(BOTH),
        P(),
        P(),
        P(),
        P(BOTH),
        P(BOTH, None),
        P("dp", "seq", None),
    )
    return jax.shard_map(
        local,
        mesh=mesh,
        in_specs=placed,
        out_specs=(
            P("dp", "seq", None),
            P("dp", "seq", None),
            P(BOTH),
            P(BOTH, None),
            P(None, BOTH),
            P(BOTH),
            P(),
            P(),
            P(),
            P(BOTH),
            P(BOTH, None),
        ),
        check_vma=False,
    )
```

```python
import jax
import jax.numpy as jnp
from jax import lax
from jax.experimental import pallas as pl
from jax.experimental.pallas import tpu as pltpu
from jax.sharding import PartitionSpec as P

D = 1536
INNER = 3072
STATE = 128
CONV = 4
HEADS = 48
CONV_CH = 3328
CHUNK = 128
GROUP = 4
BLOCK = CHUNK * GROUP
OWN = 3
WIDE = 192
PAD = 768
low = jnp.bfloat16
f32 = jnp.float32


def mm(a, b, dims=((1,), (0,))):
    return lax.dot_general(a, b, (dims, ((), ())), preferred_element_type=f32)


NT = ((1,), (1,))
TN = ((0,), (0,))


def per_head(parts):
    lane = lax.broadcasted_iota(jnp.int32, (1, WIDE), 1)
    return jnp.where(lane < 64, parts[0], jnp.where(lane < 128, parts[1], parts[2]))


def stacked(a):
    lane = lax.broadcasted_iota(jnp.int32, a.shape, 1)
    zero = jnp.zeros_like(a)
    return jnp.concatenate(
        [jnp.where((lane >= 64 * h) & (lane < 64 * h + 64), a, zero) for h in range(OWN)], axis=0
    )


def in_parts(a, count):
    parts = []
    for _ in range(count):
        parts.append(a.astype(low))
        a = a - parts[-1].astype(f32)
    return jnp.concatenate(parts, axis=0)


def summed_parts(a, count):
    n = a.shape[0] // count
    return sum([a[n * i : n * (i + 1)] for i in range(count)])


def running(a):
    s = lax.broadcasted_iota(jnp.int32, (CHUNK, CHUNK), 0)
    t = lax.broadcasted_iota(jnp.int32, (CHUNK, CHUNK), 1)
    return summed_parts(mm(in_parts(a, 3), (s <= t).astype(low)), 3)


def running_by_steps(a):
    lane = lax.broadcasted_iota(jnp.int32, a.shape, 1)
    step = 1
    while step < CHUNK:
        a = a + jnp.where(lane >= step, pltpu.roll(a, step, 1), 0.0)
        step *= 2
    return a


def reaching(after, before):
    s = lax.broadcasted_iota(jnp.int32, (2 * CHUNK, CHUNK), 0)
    t = lax.broadcasted_iota(jnp.int32, (2 * CHUNK, CHUNK), 1)
    ones = ((s < CHUNK) & (s >= t)) | ((s >= CHUNK) & (s - CHUNK < t))
    both = jnp.concatenate([after, before], axis=1)
    return summed_parts(mm(in_parts(both, 2), ones.astype(low)), 2)


def part(a, j):
    return a[CHUNK * j : CHUNK * (j + 1)]


def eight(a, j):
    return a[8 * j : 8 * (j + 1)]


def block_terms(zdt, rows_ref, head_ref, running):
    raw = jnp.concatenate([part(zdt, j)[:, 128:256].T[64:72] for j in range(GROUP)], axis=0)
    wide = lambda row: jnp.concatenate(
        [jnp.broadcast_to(rows_ref[j, row : row + 1, :], (8, CHUNK)) for j in range(GROUP)], axis=0
    )
    v = raw + head_ref[0]
    ea = jnp.exp(head_ref[1])
    step = jnp.maximum(v, 0.0) + jnp.log1p(jnp.exp(-jnp.abs(v)))
    ld = -step * ea
    cum = running(ld)
    total = cum[:, CHUNK - 1 : CHUNK]
    seg = wide(0)
    before = wide(1)[:, 0:1]
    last = seg[:, CHUNK - 1 : CHUNK]
    entry = jnp.exp(cum) * (seg == before).astype(f32)
    to_end = jnp.exp(total - cum) * (seg == last).astype(f32)
    whole = jnp.exp(total) * (last == before).astype(f32)
    leaving = to_end * step
    cols = []
    for j in range(GROUP):
        pack = [eight(cum, j), eight(entry, j), eight(leaving, j), rows_ref[j]]
        pack = jnp.concatenate(pack + [jnp.zeros((CHUNK - 32, CHUNK), f32)], axis=0)
        cols.append(pack.T)
    return v, ea, step, ld, cum, to_end, whole, cols


def barred(cols, seg):
    t = lax.broadcasted_iota(jnp.int32, (CHUNK, CHUNK), 0)
    s = lax.broadcasted_iota(jnp.int32, (CHUNK, CHUNK), 1)
    return jnp.where((t >= s) & (cols[:, 24:25] == seg), 0.0, -1e30)


def convolved(ext_ref, conv_ref):
    pre = conv_ref[CONV : CONV + 1, :]
    for k in range(CONV):
        pre = pre + conv_ref[k : k + 1, :] * ext_ref[pl.ds(5 + k, BLOCK), :]
    return pre


def forward_kernel(
    both_ref,
    w_ref,
    out_ref,
    rows_ref,
    conv_ref,
    head_ref,
    skip_ref,
    proj_ref,
    act_ref,
    slope_ref,
    z_act_ref,
    y_slope_ref,
    gated_ref,
    u_ref,
    kept_ref,
    total_ref,
    sums_ref,
    ext_ref,
    state_ref,
):
    first = pl.program_id(0) == 0

    @pl.when(first)
    def _():
        ext_ref[0:8, :] = jnp.zeros((8, 512), f32)
        state_ref[...] = jnp.zeros_like(state_ref)

    @pl.when(jnp.logical_not(first))
    def _():
        ext_ref[0:8, :] = ext_ref[BLOCK : BLOCK + 8, :]

    proj_ref[...] = mm(both_ref[:, 0:D], w_ref[...]).astype(low)
    u_ref[...] = mm(both_ref[:, D : 2 * D], out_ref[...], NT)
    zdt = proj_ref[:, 0:256].astype(f32)
    ext_ref[8 : BLOCK + 8, :] = proj_ref[:, 256:PAD].astype(f32)
    pre = convolved(ext_ref, conv_ref)
    sig = jax.nn.sigmoid(pre)
    act = pre * sig
    act_ref[...] = act.astype(low)
    slope_ref[...] = (sig + act * (1.0 - sig)).astype(low)
    x = act[:, :WIDE]
    x_low = x.astype(low)
    b_low = act[:, 256:384].astype(low)
    c_low = act[:, 384:512].astype(low)
    v, ea, step, ld, cum, to_end, whole, cols = block_terms(zdt, rows_ref, head_ref, running_by_steps)
    chunks = range(GROUP)
    scores_all = [mm(part(c_low, j), part(b_low, j), NT) for j in chunks]
    leavings = [per_head([c[:, 16 + h : 17 + h] for h in range(OWN)]) for c in cols]
    entries = [per_head([c[:, 8 + h : 9 + h] for h in range(OWN)]) for c in cols]
    wholes = [per_head([whole[8 * j + h : 8 * j + h + 1] for h in range(OWN)]) for j in chunks]
    local = [mm(part(b_low, j), (leavings[j] * part(x, j)).astype(low), TN) for j in chunks]
    mixing_all = []
    for j in chunks:
        col = cols[j]
        bar = barred(col, rows_ref[j, 0:1, :])
        mixing = []
        for h in range(OWN):
            i = 8 * j + h
            decay = jnp.exp(col[:, h : h + 1] - cum[i : i + 1] + bar)
            mixing.append((scores_all[j] * decay * step[i : i + 1]).astype(low))
        mixing_all.append(jnp.concatenate(mixing, axis=1))
    inner = [mm(mixing_all[j], stacked(part(x_low, j))) for j in chunks]
    state = state_ref[...]
    ys = []
    for j in range(GROUP):
        kept_ref[j] = state
        ys.append(inner[j] + entries[j] * mm(part(c_low, j), state.astype(low)))
        state = wholes[j] * state + local[j]
    state_ref[...] = state
    y = jnp.concatenate(ys, axis=0) + skip_ref[...] * x
    z = zdt[:, :WIDE]
    z_sig = jax.nn.sigmoid(z)
    z_act = z * z_sig
    gated = y * z_act
    gated_low = gated.astype(low)
    z_act_ref[...] = z_act.astype(low)
    y_slope_ref[...] = (y * (z_sig + z_act * (1.0 - z_sig))).astype(low)
    gated_ref[...] = gated_low
    given = mm(gated_low, out_ref[...]).astype(low)
    for j in range(GROUP):
        total_ref[j, 0] = part(given, j)
    ones = jnp.ones((8, WIDE), low)
    squares = mm(ones, (gated * gated).astype(low), NT)
    products = mm(ones, (gated * u_ref[...]).astype(low), NT)
    row = lax.broadcasted_iota(jnp.int32, (8, BLOCK), 0)
    sums_ref[...] = jnp.where(row == 0, squares, products)


def backward_kernel(
    place_ref,
    proj_ref,
    w_ref,
    both_ref,
    rows_ref,
    conv_ref,
    head_ref,
    skip_ref,
    act_ref,
    slope_ref,
    z_act_ref,
    y_slope_ref,
    gated_ref,
    u_ref,
    kept_ref,
    top_0,
    top_1,
    top_2,
    top_3,
    bottom_0,
    bottom_1,
    bottom_2,
    bottom_3,
    grads_ref,
    later_ref,
    state_ref,
    conv_grad_ref,
    head_grad_ref,
    skip_grad_ref,
    d_proj_ref,
    given_ref,
    total_ref,
    sums_ref,
):
    step_id = pl.program_id(0)
    count = pl.num_programs(0)

    @pl.when(step_id == 0)
    def _():
        later_ref[BLOCK : BLOCK + 8, :] = jnp.zeros((8, 512), f32)
        state_ref[...] = jnp.zeros_like(state_ref)
        conv_grad_ref[...] = jnp.zeros_like(conv_grad_ref)
        head_grad_ref[...] = jnp.zeros_like(head_grad_ref)
        skip_grad_ref[...] = jnp.zeros_like(skip_grad_ref)
        total_ref[...] = jnp.zeros_like(total_ref)

    @pl.when(step_id > 0)
    def _():
        later_ref[BLOCK : BLOCK + 8, :] = later_ref[0:8, :]

    conv_in = proj_ref[:, 256:PAD].astype(f32)
    zdt = proj_ref[:, 0:256].astype(f32)
    x_low = act_ref[:, :WIDE]
    x = x_low.astype(f32)
    b_low = act_ref[:, 256:384]
    c_low = act_ref[:, 384:512]
    v, ea, step, ld, cum, to_end, whole, cols = block_terms(zdt, rows_ref, head_ref, running)

    r_col = jnp.concatenate([c[:, 26:27] for c in cols], axis=0)
    c_col = jnp.concatenate([c[:, 27:28] for c in cols], axis=0)
    gated = gated_ref[...].astype(f32)
    d_gated = r_col * u_ref[...] - c_col * gated
    dy = d_gated * z_act_ref[...].astype(f32)
    dz = d_gated * y_slope_ref[...].astype(f32)
    dy_low = dy.astype(low)
    normed = (gated * r_col).astype(low)
    out_grad = mm(normed, both_ref[:, D : 2 * D], TN)
    for d in range(8):
        total_ref[d, 192:216] += out_grad[24 * d : 24 * d + 24, 0:PAD]
        total_ref[d, 216:240] += out_grad[24 * d : 24 * d + 24, PAD:D]

    t = lax.broadcasted_iota(jnp.int32, (CHUNK, CHUNK), 0)
    s = lax.broadcasted_iota(jnp.int32, (CHUNK, CHUNK), 1)
    earlier = (t < s).astype(low)
    blank = jnp.zeros((8 - OWN, CHUNK), f32)
    row_head = lax.broadcasted_iota(jnp.int32, (8, WIDE), 0)
    lane = lax.broadcasted_iota(jnp.int32, (8, WIDE), 1)
    by_head = ((lane >= 64 * row_head) & (lane < 64 * row_head + 64)).astype(low)

    chunks = range(GROUP)
    d_scores_all, d_steps_all, inside_all, mixing_all, flow_all = [], [], [], [], []
    entries = [per_head([c[:, 8 + h : 9 + h] for h in range(OWN)]) for c in cols]
    leavings = [per_head([c[:, 16 + h : 17 + h] for h in range(OWN)]) for c in cols]
    wholes = [per_head([whole[8 * j + h : 8 * j + h + 1] for h in range(OWN)]) for j in chunks]
    scores_all = [mm(part(c_low, j), part(b_low, j), NT) for j in chunks]
    d_mixing_all = [mm(part(dy_low, j), stacked(part(x_low, j)), NT) for j in chunks]
    dy_entries = [entries[j] * part(dy, j) for j in chunks]
    to_state = [mm(part(c_low, j), dy_entries[j].astype(low), TN) for j in chunks]
    for j in chunks:
        col = cols[j]
        bar = barred(col, rows_ref[j, 0:1, :])
        scores, d_mixing = scores_all[j], d_mixing_all[j]
        d_scores = jnp.zeros((CHUNK, CHUNK), f32)
        mixings, flows, d_steps = [], [], []
        for h in range(OWN):
            i = 8 * j + h
            decay = jnp.exp(col[:, h : h + 1] - cum[i : i + 1] + bar)
            stepped = decay * step[i : i + 1]
            mixing = scores * stepped
            mixings.append(mixing.astype(low))
            d_mix = d_mixing[:, CHUNK * h : CHUNK * h + CHUNK]
            d_scores = d_scores + d_mix * stepped
            flows.append((d_mix * mixing).astype(low))
            d_steps.append(jnp.sum(d_mix * scores * decay, axis=0, keepdims=True))
        d_scores_all.append(d_scores.astype(low))
        d_steps_all += d_steps + [blank]
        mixing_all.append(jnp.concatenate(mixings, axis=0))
        flow_all.append(jnp.concatenate(flows, axis=0))
    reach_all = [mm(flow_all[j], earlier) for j in chunks]
    dx_in = [mm(mixing_all[j], stacked(part(dy_low, j)), TN) for j in chunks]
    for j in chunks:
        inside_all += [
            jnp.sum(jnp.where(t >= s, part(reach_all[j], h), 0.0), axis=0, keepdims=True)
            for h in range(OWN)
        ] + [blank]

    laters = [None] * GROUP
    later = state_ref[...]
    for j in reversed(range(GROUP)):
        laters[j] = later
        later = wholes[j] * later + to_state[j]
    state_ref[...] = later

    bs = [part(b_low, j) for j in chunks]
    cs = [part(c_low, j) for j in chunks]
    states = [kept_ref[j] for j in chunks]
    state_lows = [a.astype(low) for a in states]
    later_lows = [a.astype(low) for a in laters]
    from_laters = [mm(bs[j], later_lows[j]) for j in chunks]
    from_states = [mm(cs[j], state_lows[j]) for j in chunks]
    dc_in = [mm(d_scores_all[j], bs[j]) for j in chunks]
    db_in = [mm(d_scores_all[j], cs[j], TN) for j in chunks]
    dc_out = [mm(dy_entries[j].astype(low), state_lows[j], NT) for j in chunks]
    db_out = [
        mm((leavings[j] * part(x, j)).astype(low), later_lows[j], NT) for j in chunks
    ]
    xv = [mm(by_head, (part(x, j) * from_laters[j]).astype(low), NT) for j in chunks]
    row_state = [mm(by_head, (dy_entries[j] * from_states[j]).astype(low), NT) for j in chunks]
    overlap = [
        jnp.sum(mm(by_head, (laters[j] * states[j]).astype(low), NT), axis=1, keepdims=True)
        for j in chunks
    ]
    dxs = [dx_in[j] + leavings[j] * from_laters[j] for j in chunks]
    dcs = [dc_in[j] + dc_out[j] for j in chunks]
    dbs = [db_in[j] + db_out[j] for j in chunks]
    stack = lambda a: jnp.concatenate(a, axis=0)
    ended = to_end * stack(xv)
    col_state = ended * step
    d_step = stack(d_steps_all) + ended
    d_ld = (
        stack(inside_all)
        + reaching(stack(row_state), col_state)
        + whole * stack(overlap)
    )
    d_dt = (d_step - d_ld * ea) * jax.nn.sigmoid(v)
    head_grad_ref[0] += sum([eight(d_dt, j) for j in range(GROUP)])
    head_grad_ref[1] += sum([eight(d_ld * ld, j) for j in range(GROUP)])
    skip_grad_ref[...] += jnp.sum((dy * x).reshape(BLOCK // 8, 8, WIDE), axis=0)

    dx = stack(dxs) + skip_ref[...] * dy
    later_ref[0:BLOCK, 0:WIDE] = dx * slope_ref[:, :WIDE].astype(f32)
    later_ref[0:BLOCK, WIDE:256] = jnp.zeros((BLOCK, 256 - WIDE), f32)
    later_ref[0:BLOCK, 256:384] = stack(dbs) * slope_ref[:, 256:384].astype(f32)
    later_ref[0:BLOCK, 384:512] = stack(dcs) * slope_ref[:, 384:512].astype(f32)
    d_conv_in = jnp.zeros((BLOCK, 512), f32)
    for k in range(CONV):
        moved = later_ref[pl.ds(CONV - 1 - k, BLOCK), :]
        d_conv_in = d_conv_in + conv_ref[k : k + 1, :] * moved
        conv_grad_ref[k] += jnp.sum((moved * conv_in).reshape(BLOCK // 8, 8, 512), axis=0)
        if k == CONV - 1:
            conv_grad_ref[CONV] += jnp.sum(moved.reshape(BLOCK // 8, 8, 512), axis=0)

    turned = []
    for j in range(GROUP):
        tall = [jnp.zeros((64, CHUNK), f32), eight(d_dt, j), jnp.zeros((56, CHUNK), f32)]
        turned.append(jnp.concatenate(tall, axis=0).T)
    d_proj_ref[:, 0:128] = dz[:, 0:128].astype(low)
    d_proj_ref[:, 128:256] = jnp.concatenate(
        [dz[:, 128:WIDE], stack(turned)[:, 64:128]], axis=1
    ).astype(low)
    d_proj_ref[:, 256:PAD] = d_conv_in.astype(low)

    in_grad = mm(both_ref[:, 0:D], d_proj_ref[...], TN)
    for d in range(8):
        total_ref[d, 0:192] += in_grad[192 * d : 192 * d + 192]
    given_ref[...] = mm(d_proj_ref[...], w_ref[...], NT).astype(low)

    row = count - 1 - step_id
    up = lax.rem(row - place_ref[1] + 4, 4)
    for k, ref in enumerate((top_0, top_1, top_2, top_3)):

        @pl.when(up == k)
        def _():
            for j in range(GROUP):
                ref[j] = given_ref[CHUNK * j : CHUNK * j + 64, :]

    for k, ref in enumerate((bottom_0, bottom_1, bottom_2, bottom_3)):
        for j in range(GROUP):

            @pl.when(lax.rem(j - place_ref[0] + 4, 4) == k)
            def _():
                ref[row] = given_ref[CHUNK * j + 64 : CHUNK * (j + 1), :]

    @pl.when(step_id == count - 1)
    def _():
        lane = lax.broadcasted_iota(jnp.int32, (8, 256), 1)
        head = lax.broadcasted_iota(jnp.int32, (8, 256), 0)
        bias = jnp.sum(head_grad_ref[0], axis=1, keepdims=True)
        rate = jnp.sum(head_grad_ref[1], axis=1, keepdims=True)
        heads = jnp.where((lane == head) & (head < OWN), bias, 0.0)
        heads = heads + jnp.where((lane == head + OWN) & (head < OWN), rate, 0.0)
        taps = [jnp.sum(conv_grad_ref[k], axis=0, keepdims=True) for k in range(CONV + 1)]
        skips = jnp.sum(skip_grad_ref[...], axis=0, keepdims=True)
        for k in range(CONV):
            sums_ref[k : k + 1, 0:512] = taps[k]
        sums_ref[0:1, 512:PAD] = taps[CONV][:, 0:256]
        sums_ref[1:2, 512:PAD] = taps[CONV][:, 256:512]
        sums_ref[2:3, 512 : 512 + WIDE] = skips
        sums_ref[2:3, 512 + WIDE : PAD] = jnp.zeros((1, 256 - WIDE), f32)
        sums_ref[3:4, 512:PAD] = jnp.sum(heads, axis=0, keepdims=True)
        high = sums_ref[0:4, :].astype(low).astype(f32)
        tail = jnp.concatenate([high, sums_ref[0:4, :] - high], axis=0)
        for d in range(8):
            grads_ref[d] = jnp.concatenate([total_ref[d], tail], axis=0).astype(low)


def ssd_forward(both, w, w_out, rows, conv, heads, skip):
    length = both.shape[0]
    steps = length // BLOCK
    whole = lambda shape: pl.BlockSpec(shape, lambda i: (0,) * len(shape))
    here = lambda width: pl.BlockSpec((BLOCK, width), lambda i: (i, 0))
    return pl.pallas_call(
        forward_kernel,
        grid=(steps,),
        in_specs=[
            here(2 * D),
            whole((D, PAD)),
            whole((WIDE, D)),
            pl.BlockSpec((GROUP, 8, CHUNK), lambda i: (i, 0, 0)),
            whole((8, 512)),
            whole((2, 8 * GROUP, CHUNK)),
            whole((1, WIDE)),
        ],
        out_specs=[
            here(PAD),
            here(512),
            here(512),
            here(WIDE),
            here(WIDE),
            here(WIDE),
            here(WIDE),
            pl.BlockSpec((GROUP, STATE, WIDE), lambda i: (i, 0, 0)),
            pl.BlockSpec((GROUP, 1, CHUNK, D), lambda i: (0, i, 0, 0)),
            pl.BlockSpec((8, BLOCK), lambda i: (0, i)),
        ],
        out_shape=[
            jax.ShapeDtypeStruct((length, PAD), low),
            jax.ShapeDtypeStruct((length, 512), low),
            jax.ShapeDtypeStruct((length, 512), low),
            jax.ShapeDtypeStruct((length, WIDE), low),
            jax.ShapeDtypeStruct((length, WIDE), low),
            jax.ShapeDtypeStruct((length, WIDE), low),
            jax.ShapeDtypeStruct((length, WIDE), f32),
            jax.ShapeDtypeStruct((length // CHUNK, STATE, WIDE), f32),
            jax.ShapeDtypeStruct((GROUP, steps, CHUNK, D), low),
            jax.ShapeDtypeStruct((8, length), f32),
        ],
        scratch_shapes=[pltpu.VMEM((BLOCK + 8, 512), f32), pltpu.VMEM((STATE, WIDE), f32)],
        compiler_params=pltpu.CompilerParams(
            dimension_semantics=("arbitrary",), vmem_limit_bytes=56 * 1024 * 1024
        ),
        name="ssd_forward",
    )(both, w, w_out, rows, conv, heads, skip)


def ssd_backward(place, both, w, proj, rows, conv, heads, skip, *saved):
    length = proj.shape[0]
    steps = length // BLOCK
    back = lambda i: steps - 1 - i
    whole = lambda shape: pl.BlockSpec(shape, lambda i: (0,) * len(shape))
    here = lambda width: pl.BlockSpec((BLOCK, width), lambda i: (back(i), 0))
    return pl.pallas_call(
        backward_kernel,
        grid=(steps,),
        in_specs=[
            pl.BlockSpec(memory_space=pltpu.SMEM),
            here(PAD),
            whole((D, PAD)),
            here(2 * D),
            pl.BlockSpec((GROUP, 8, CHUNK), lambda i: (back(i), 0, 0)),
            whole((8, 512)),
            whole((2, 8 * GROUP, CHUNK)),
            whole((1, WIDE)),
            here(512),
            here(512),
            here(WIDE),
            here(WIDE),
            here(WIDE),
            here(WIDE),
            pl.BlockSpec((GROUP, STATE, WIDE), lambda i: (back(i), 0, 0)),
        ],
        out_specs=[
            *[whole((4, 64, D)) for _ in range(8)],
            whole((8, 248, PAD)),
        ],
        out_shape=[
            *[jax.ShapeDtypeStruct((4, 64, D), low) for _ in range(8)],
            jax.ShapeDtypeStruct((8, 248, PAD), low),
        ],
        scratch_shapes=[
            pltpu.VMEM((BLOCK + 8, 512), f32),
            pltpu.VMEM((STATE, WIDE), f32),
            pltpu.VMEM((CONV + 1, 8, 512), f32),
            pltpu.VMEM((2, 8, CHUNK), f32),
            pltpu.VMEM((8, WIDE), f32),
            pltpu.VMEM((BLOCK, PAD), low),
            pltpu.VMEM((BLOCK, D), low),
            pltpu.VMEM((8, 240, PAD), f32),
            pltpu.VMEM((8, PAD), f32),
        ],
        compiler_params=pltpu.CompilerParams(
            dimension_semantics=("arbitrary",), vmem_limit_bytes=56 * 1024 * 1024
        ),
        name="ssd_backward",
    )(place, proj, w, both, rows, conv, heads, skip, *saved)


epsilon = 1e-05
BOTH = ("dp", "seq")
X_GROUPS = [[4 * y + x for x in range(4)] for y in range(4)]
Y_GROUPS = [[4 * y + x for y in range(4)] for x in range(4)]


def columns_of(a, small):
    rows = a.shape[0]
    z = a[:, :INNER].reshape(rows, 16, WIDE)
    x = a[:, INNER : 2 * INNER].reshape(rows, 16, WIDE)
    bc = jnp.broadcast_to(a[:, None, 2 * INNER : 2 * INNER + 256], (rows, 16, 256))
    dt = a[:, 2 * INNER + 256 :].reshape(rows, 16, OWN)
    blank = lambda n: jnp.zeros((rows, 16, n), a.dtype)
    small = jnp.broadcast_to(small[:, None], (rows, 16, 22))
    return jnp.concatenate([z, dt, blank(61), x, small, blank(42), bc], axis=2).transpose(1, 0, 2)


def padded(a):
    return jnp.concatenate(
        [a[:, :WIDE], jnp.zeros((a.shape[0], 64), a.dtype), a[:, WIDE:]], axis=1
    )


def along_x(a, k):
    return lax.ppermute(a, "seq", [(s, (s // 4) * 4 + (s % 4 + k) % 4) for s in range(16)])


def along_y(a, k):
    return lax.ppermute(a, "seq", [(s, ((s // 4 + k) % 4) * 4 + s % 4) for s in range(16)])


def along_z(a, k):
    return lax.ppermute(a, "dp", [(d, ((d // 2 + k) % 4) * 2 + d % 2) for d in range(8)])


def other_core(a):
    return lax.ppermute(a, "dp", [(d, d ^ 1) for d in range(8)])


def put(buf, piece, *at):
    return lax.dynamic_update_slice(buf, piece, tuple(at) + (0,) * (buf.ndim - len(at)))


def take(a, i):
    return lax.dynamic_index_in_dim(a, i % a.shape[0], 0, False)


def added(a, b):
    return (a.astype(f32) + b.astype(f32)).astype(low)


def ring_sum(block, along, wait):
    h = block[2].shape[0] // 2
    from_up, from_down = wait((along(block[2][:h], 1), along(block[2][h:], 3)))
    up = jnp.concatenate([added(block[1][:h], from_up), block[1][h:]], axis=0)
    down = jnp.concatenate([block[3][:h], added(block[3][h:], from_down)], axis=0)
    up, down = along(up, 1), along(down, 3)
    return block[0].astype(f32) + up.astype(f32) + down.astype(f32)


def scattered_sum(top, bottom):
    me = lax.axis_index("seq")
    x, y = me % 4, me // 4
    total = lambda own, sent: sum([s.astype(f32) for s in sent], own.astype(f32))
    came = []

    def wait(pieces):
        came.extend(pieces)
        return pieces

    top = ring_sum(top, along_y, wait).astype(low)
    bottom = ring_sum(bottom, along_x, wait).astype(low)
    own_top = total(take(top, x), [along_x(take(top, x + k), k) for k in (2, 1, 3)])
    own_bottom = total(take(bottom, y), [along_y(take(bottom, y + k), k) for k in (2, 1, 3)])
    return jnp.concatenate([own_top, own_bottom], axis=0), came


def gathered_z(a):
    d = lax.axis_index("dp")
    z, core = d // 2, d % 2
    h = a.shape[0] // 2
    first, last = a[:h], a[h:]
    up_first = along_z(first, 1)
    down_last = along_z(last, 3)
    up_last = along_z(last, 1)
    down_first = along_z(first, 3)
    far_first = along_z(up_first, 1)
    far_last = along_z(down_last, 3)
    mine = put(jnp.zeros((4, 2, h, a.shape[1]), a.dtype), a.reshape(1, 2, h, -1), z)
    for k, p, q in ((3, up_first, up_last), (1, down_first, down_last), (2, far_first, far_last)):
        mine = put(mine, p[None, None], (z + k) % 4, 0)
        mine = put(mine, q[None, None], (z + k) % 4, 1)
    mine = mine.reshape(4, 1, 2 * h, -1)
    other = other_core(mine)
    first = core == 0
    pair = (jnp.where(first, mine, other), jnp.where(first, other, mine))
    return jnp.concatenate(pair, axis=1).reshape(8, 2 * h, -1)


def seq_sum(a):
    a = a + along_x(a, 1) + along_x(a, 3) + along_x(a, 2)
    return a + along_y(a, 1) + along_y(a, 3) + along_y(a, 2)


def block_order(back):
    pairs = [(f, (f % 8) * 16 + f // 8) for f in range(128)]
    return [(b, a) for a, b in pairs] if back else pairs


def local(
    hidden,
    segments,
    pre_gain,
    w_in,
    conv_weight,
    conv_bias,
    dt_bias,
    a_log,
    d_skip,
    gate_gain,
    w_out,
    grad_out,
):
    me = lax.axis_index("seq")
    row = lax.axis_index("dp")
    tokens = hidden[0].astype(f32)
    r0 = lax.rsqrt(jnp.mean(tokens * tokens, axis=-1, keepdims=True) + epsilon)
    hn = (tokens * r0).astype(low)
    both = jnp.concatenate([hn, grad_out[0]], axis=1)
    both = lax.all_gather(both, "seq", axis=0, tiled=True)

    gain_in = pre_gain.astype(f32)[:, None]
    gain_out = gate_gain.astype(f32)[:, None]
    w_in_wide = w_in.astype(f32)
    w_out_wide = w_out.astype(f32)
    small = jnp.concatenate([conv_weight.reshape(-1), conv_bias, segments[0].astype(low)])
    small = jnp.pad(small, (0, 264 - small.shape[0])).reshape(12, 22)
    parts = columns_of((w_in_wide * gain_in).astype(low), small).reshape(16 * 12, PAD)
    parts = lax.all_to_all(parts, "seq", 0, 0, tiled=True)
    segment = parts[:, 448:470].reshape(16, 264)[:, 130:258].astype(f32).reshape(1, 2048)
    before = jnp.concatenate([jnp.full((1, 1), -1.0, f32), segment[:, :-1]], axis=1)
    blocks = lax.ppermute((w_out_wide * gain_out).astype(low), BOTH, block_order(False))
    weights = gathered_z(jnp.concatenate([parts, blocks.reshape(48, PAD)], axis=0))
    w_own = weights[:, :192].reshape(D, PAD)
    w_out_own = weights[:, 192:].reshape(WIDE, D)
    conv_all = weights[:, :192, 448:470].reshape(128, 264)[:, :130].astype(f32)
    conv_all = conv_all.reshape(128, 5, 26).transpose(1, 0, 2).reshape(5, CONV_CH)
    conv = jnp.concatenate(
        [lax.dynamic_slice_in_dim(conv_all, me * WIDE, WIDE, 1), conv_all[:, INNER:]], axis=1
    )
    conv = jnp.concatenate([padded(conv), jnp.zeros((3, 512), f32)], axis=0)
    own = lambda a: lax.dynamic_slice_in_dim(a, me * OWN, OWN, 0)
    tall = lambda a: jnp.broadcast_to(
        jnp.tile(jnp.pad(own(a), (0, 8 - OWN)), GROUP)[:, None], (8 * GROUP, CHUNK)
    )
    heads = jnp.stack([tall(dt_bias), tall(a_log)])
    skip = jnp.repeat(own(d_skip), 64)[None]
    by_chunk = lambda rows: jnp.concatenate(
        rows + [jnp.zeros((8 - len(rows), 2048), f32)], axis=0
    ).reshape(8, 16, CHUNK).transpose(1, 0, 2)

    proj, *saved, partial_out, sums = ssd_forward(
        both, w_own, w_out_own, by_chunk([segment, before]), conv, heads, skip
    )
    total = lax.psum_scatter(
        partial_out.reshape(2048, D), "seq", scatter_dimension=0, tiled=True, axis_index_groups=X_GROUPS
    )
    sums = seq_sum(sums[:2].reshape(32, 128)).reshape(2, 2048)
    r = lax.rsqrt(sums[0:1] / INNER + epsilon)
    c = r * r * r * (sums[1:2] / INNER)

    place = jnp.stack([me % 4, me // 4])
    *pieces, grads = ssd_backward(
        place, both, w_own, proj, by_chunk([segment, before, r, c]), conv, heads, skip, *saved
    )
    v, came = scattered_sum(pieces[:4], pieces[4:])
    grads, total = lax.optimization_barrier((grads, total))
    grads = lax.psum_scatter(grads.reshape(8 * 248, PAD), "dp", scatter_dimension=0, tiled=True)
    grads, total = lax.optimization_barrier((grads, total))
    total = lax.psum_scatter(
        total, "seq", scatter_dimension=0, tiled=True, axis_index_groups=Y_GROUPS
    )
    small = (grads[240:244].astype(f32) + grads[244:248].astype(f32)).astype(low)
    g_parts = jnp.concatenate(
        [grads[:192].reshape(16, 12, PAD), jnp.broadcast_to(small[None], (16, 4, PAD))], axis=1
    )
    g_parts = lax.all_to_all(g_parts, "seq", 0, 0)
    g_out = lax.ppermute(grads[192:240], BOTH, block_order(True)).astype(f32)
    g_out = jnp.concatenate([g_out[:24], g_out[24:]], axis=1)
    small = g_parts[:, 12:].astype(f32)
    g_parts = g_parts[:, :12]
    conv_sum = jnp.concatenate(
        [
            small[:, :, :WIDE].transpose(1, 0, 2).reshape(CONV, INNER),
            jnp.sum(small[:, :, 256:512], axis=0),
        ],
        axis=1,
    )
    bias_sum = jnp.concatenate(
        [small[:, 0, 512 : 512 + WIDE].reshape(INNER), jnp.sum(small[:, 1, 512:], axis=0)]
    )
    at = 26 * (16 * row + me)
    conv_sum = lax.dynamic_slice_in_dim(conv_sum, at, 26, 1)
    bias_sum = lax.dynamic_slice_in_dim(bias_sum, at, 26, 0)
    head_sum = (
        small[:, 3, 512 : 512 + OWN].reshape(HEADS),
        small[:, 3, 512 + OWN : 512 + 2 * OWN].reshape(HEADS),
        small[:, 2, 512 : 512 + WIDE].reshape(HEADS, 64).sum(axis=1),
    )
    g_parts = g_parts.astype(f32).transpose(1, 0, 2)
    g_in = jnp.concatenate(
        [
            g_parts[:, :, :WIDE].reshape(12, INNER),
            g_parts[:, :, 256 : 256 + WIDE].reshape(12, INNER),
            jnp.sum(g_parts[:, :, 512:], axis=1),
            g_parts[:, :, WIDE : WIDE + OWN].reshape(12, HEADS),
        ],
        axis=1,
    )
    grad_w_in = gain_in * g_in
    grad_pre_gain = jnp.sum(w_in_wide * g_in, axis=1)
    grad_w_out = gain_out * g_out
    grad_gate_gain = jnp.sum(w_out_wide * g_out, axis=1)
    r_own = lax.dynamic_slice_in_dim(r[0], me * 128, 128, 0)
    block_out = (r_own[:, None] * total.astype(f32) + tokens).astype(low)
    mean = jnp.mean(v * tokens, axis=-1, keepdims=True)
    grad_hidden = (
        grad_out[0].astype(f32) + r0 * v - tokens * (r0 * r0 * r0 * mean)
    ).astype(low)
    return (
        block_out[None],
        grad_hidden[None],
        grad_pre_gain,
        grad_w_in,
        conv_sum,
        bias_sum,
        head_sum[0],
        head_sum[1],
        head_sum[2],
        grad_gate_gain,
        grad_w_out,
    )


def solution(mesh):
    placed = (
        P("dp", "seq", None),
        P("dp", "seq"),
        P(BOTH),
        P(BOTH, None),
        P(None, BOTH),
        P(BOTH),
        P(),
        P(),
        P(),
        P(BOTH),
        P(BOTH, None),
        P("dp", "seq", None),
    )
    return jax.shard_map(
        local,
        mesh=mesh,
        in_specs=placed,
        out_specs=(
            P("dp", "seq", None),
            P("dp", "seq", None),
            P(BOTH),
            P(BOTH, None),
            P(None, BOTH),
            P(BOTH),
            P(),
            P(),
            P(),
            P(BOTH),
            P(BOTH, None),
        ),
        check_vma=False,
    )
```

```python
import jax
import jax.numpy as jnp
from jax import lax
from jax.experimental import pallas as pl
from jax.experimental.pallas import tpu as pltpu
from jax.sharding import PartitionSpec as P

D = 1536
INNER = 3072
STATE = 128
CONV = 4
HEADS = 48
HEADDIM = 64
CONV_CH = 3328
CHUNK = 128
GROUP = 4
BLOCK = CHUNK * GROUP
OWN = 3
WIDE = 192
PAD = 768
low = jnp.bfloat16
f32 = jnp.float32


def mm(a, b, dims=((1,), (0,))):
    return lax.dot_general(a, b, (dims, ((), ())), preferred_element_type=f32)


NT = ((1,), (1,))
TN = ((0,), (0,))


def per_head(parts):
    lane = lax.broadcasted_iota(jnp.int32, (1, WIDE), 1)
    return jnp.where(lane < 64, parts[0], jnp.where(lane < 128, parts[1], parts[2]))


def stacked(a):
    lane = lax.broadcasted_iota(jnp.int32, a.shape, 1)
    zero = jnp.zeros_like(a)
    return jnp.concatenate(
        [jnp.where((lane >= 64 * h) & (lane < 64 * h + 64), a, zero) for h in range(OWN)], axis=0
    )


def in_parts(a, count):
    parts = []
    for _ in range(count):
        parts.append(a.astype(low))
        a = a - parts[-1].astype(f32)
    return jnp.concatenate(parts, axis=0)


def summed_parts(a, count):
    n = a.shape[0] // count
    return sum([a[n * i : n * (i + 1)] for i in range(count)])


def running(a):
    s = lax.broadcasted_iota(jnp.int32, (CHUNK, CHUNK), 0)
    t = lax.broadcasted_iota(jnp.int32, (CHUNK, CHUNK), 1)
    return summed_parts(mm(in_parts(a, 3), (s <= t).astype(low)), 3)


def running_by_steps(a):
    lane = lax.broadcasted_iota(jnp.int32, a.shape, 1)
    step = 1
    while step < CHUNK:
        a = a + jnp.where(lane >= step, pltpu.roll(a, step, 1), 0.0)
        step *= 2
    return a


def reaching(after, before):
    s = lax.broadcasted_iota(jnp.int32, (2 * CHUNK, CHUNK), 0)
    t = lax.broadcasted_iota(jnp.int32, (2 * CHUNK, CHUNK), 1)
    ones = ((s < CHUNK) & (s >= t)) | ((s >= CHUNK) & (s - CHUNK < t))
    both = jnp.concatenate([after, before], axis=1)
    return summed_parts(mm(in_parts(both, 2), ones.astype(low)), 2)


def part(a, j):
    return a[CHUNK * j : CHUNK * (j + 1)]


def eight(a, j):
    return a[8 * j : 8 * (j + 1)]


def block_terms(zdt, rows_ref, head_ref, running):
    raw = jnp.concatenate([part(zdt, j)[:, 128:256].T[64:72] for j in range(GROUP)], axis=0)
    wide = lambda row: jnp.concatenate(
        [jnp.broadcast_to(rows_ref[j, row : row + 1, :], (8, CHUNK)) for j in range(GROUP)], axis=0
    )
    v = raw + head_ref[0]
    ea = jnp.exp(head_ref[1])
    step = jnp.maximum(v, 0.0) + jnp.log1p(jnp.exp(-jnp.abs(v)))
    ld = -step * ea
    cum = running(ld)
    total = cum[:, CHUNK - 1 : CHUNK]
    seg = wide(0)
    before = wide(1)[:, 0:1]
    last = seg[:, CHUNK - 1 : CHUNK]
    entry = jnp.exp(cum) * (seg == before).astype(f32)
    to_end = jnp.exp(total - cum) * (seg == last).astype(f32)
    whole = jnp.exp(total) * (last == before).astype(f32)
    leaving = to_end * step
    cols = []
    for j in range(GROUP):
        pack = [eight(cum, j), eight(entry, j), eight(leaving, j), rows_ref[j]]
        pack = jnp.concatenate(pack + [jnp.zeros((CHUNK - 32, CHUNK), f32)], axis=0)
        cols.append(pack.T)
    return v, ea, step, ld, cum, to_end, whole, cols


def barred(cols, seg):
    t = lax.broadcasted_iota(jnp.int32, (CHUNK, CHUNK), 0)
    s = lax.broadcasted_iota(jnp.int32, (CHUNK, CHUNK), 1)
    return jnp.where((t >= s) & (cols[:, 24:25] == seg), 0.0, -1e30)


def convolved(ext_ref, conv_ref):
    pre = conv_ref[CONV : CONV + 1, :]
    for k in range(CONV):
        pre = pre + conv_ref[k : k + 1, :] * ext_ref[pl.ds(5 + k, BLOCK), :]
    return pre


def forward_kernel(
    both_ref,
    w_ref,
    out_ref,
    rows_ref,
    conv_ref,
    head_ref,
    skip_ref,
    proj_ref,
    act_ref,
    slope_ref,
    z_act_ref,
    y_slope_ref,
    gated_ref,
    u_ref,
    kept_ref,
    total_ref,
    sums_ref,
    ext_ref,
    state_ref,
):
    first = pl.program_id(0) == 0

    @pl.when(first)
    def _():
        ext_ref[0:8, :] = jnp.zeros((8, 512), f32)
        state_ref[...] = jnp.zeros_like(state_ref)

    @pl.when(jnp.logical_not(first))
    def _():
        ext_ref[0:8, :] = ext_ref[BLOCK : BLOCK + 8, :]

    proj_ref[...] = mm(both_ref[:, 0:D], w_ref[...]).astype(low)
    u_ref[...] = mm(both_ref[:, D : 2 * D], out_ref[...], NT)
    zdt = proj_ref[:, 0:256].astype(f32)
    ext_ref[8 : BLOCK + 8, :] = proj_ref[:, 256:PAD].astype(f32)
    pre = convolved(ext_ref, conv_ref)
    sig = jax.nn.sigmoid(pre)
    act = pre * sig
    act_ref[...] = act.astype(low)
    slope_ref[...] = (sig + act * (1.0 - sig)).astype(low)
    x = act[:, :WIDE]
    x_low = x.astype(low)
    b_low = act[:, 256:384].astype(low)
    c_low = act[:, 384:512].astype(low)
    v, ea, step, ld, cum, to_end, whole, cols = block_terms(zdt, rows_ref, head_ref, running_by_steps)
    chunks = range(GROUP)
    scores_all = [mm(part(c_low, j), part(b_low, j), NT) for j in chunks]
    leavings = [per_head([c[:, 16 + h : 17 + h] for h in range(OWN)]) for c in cols]
    entries = [per_head([c[:, 8 + h : 9 + h] for h in range(OWN)]) for c in cols]
    wholes = [per_head([whole[8 * j + h : 8 * j + h + 1] for h in range(OWN)]) for j in chunks]
    local = [mm(part(b_low, j), (leavings[j] * part(x, j)).astype(low), TN) for j in chunks]
    mixing_all = []
    for j in chunks:
        col = cols[j]
        bar = barred(col, rows_ref[j, 0:1, :])
        mixing = []
        for h in range(OWN):
            i = 8 * j + h
            decay = jnp.exp(col[:, h : h + 1] - cum[i : i + 1] + bar)
            mixing.append((scores_all[j] * decay * step[i : i + 1]).astype(low))
        mixing_all.append(jnp.concatenate(mixing, axis=1))
    inner = [mm(mixing_all[j], stacked(part(x_low, j))) for j in chunks]
    state = state_ref[...]
    ys = []
    for j in range(GROUP):
        kept_ref[j] = state
        ys.append(inner[j] + entries[j] * mm(part(c_low, j), state.astype(low)))
        state = wholes[j] * state + local[j]
    state_ref[...] = state
    y = jnp.concatenate(ys, axis=0) + skip_ref[...] * x
    z = zdt[:, :WIDE]
    z_sig = jax.nn.sigmoid(z)
    z_act = z * z_sig
    gated = y * z_act
    gated_low = gated.astype(low)
    z_act_ref[...] = z_act.astype(low)
    y_slope_ref[...] = (y * (z_sig + z_act * (1.0 - z_sig))).astype(low)
    gated_ref[...] = gated_low
    given = mm(gated_low, out_ref[...]).astype(low)
    for j in range(GROUP):
        total_ref[j, 0] = part(given, j)
    ones = jnp.ones((8, WIDE), low)
    squares = mm(ones, (gated * gated).astype(low), NT)
    products = mm(ones, (gated * u_ref[...]).astype(low), NT)
    row = lax.broadcasted_iota(jnp.int32, (8, BLOCK), 0)
    sums_ref[...] = jnp.where(row == 0, squares, products)


def backward_kernel(
    place_ref,
    proj_ref,
    w_ref,
    both_ref,
    rows_ref,
    conv_ref,
    head_ref,
    skip_ref,
    act_ref,
    slope_ref,
    z_act_ref,
    y_slope_ref,
    gated_ref,
    u_ref,
    kept_ref,
    top_0,
    top_1,
    top_2,
    top_3,
    bottom_0,
    bottom_1,
    bottom_2,
    bottom_3,
    grads_ref,
    others_ref,
    later_ref,
    state_ref,
    conv_grad_ref,
    head_grad_ref,
    skip_grad_ref,
    d_proj_ref,
    given_ref,
    total_ref,
    sums_ref,
):
    step_id = pl.program_id(0)
    count = pl.num_programs(0)

    @pl.when(step_id == 0)
    def _():
        later_ref[BLOCK : BLOCK + 8, :] = jnp.zeros((8, 512), f32)
        state_ref[...] = jnp.zeros_like(state_ref)
        conv_grad_ref[...] = jnp.zeros_like(conv_grad_ref)
        head_grad_ref[...] = jnp.zeros_like(head_grad_ref)
        skip_grad_ref[...] = jnp.zeros_like(skip_grad_ref)
        total_ref[...] = jnp.zeros_like(total_ref)

    @pl.when(step_id > 0)
    def _():
        later_ref[BLOCK : BLOCK + 8, :] = later_ref[0:8, :]

    conv_in = proj_ref[:, 256:PAD].astype(f32)
    zdt = proj_ref[:, 0:256].astype(f32)
    x_low = act_ref[:, :WIDE]
    x = x_low.astype(f32)
    b_low = act_ref[:, 256:384]
    c_low = act_ref[:, 384:512]
    v, ea, step, ld, cum, to_end, whole, cols = block_terms(zdt, rows_ref, head_ref, running)

    r_col = jnp.concatenate([c[:, 26:27] for c in cols], axis=0)
    c_col = jnp.concatenate([c[:, 27:28] for c in cols], axis=0)
    gated = gated_ref[...].astype(f32)
    d_gated = r_col * u_ref[...] - c_col * gated
    dy = d_gated * z_act_ref[...].astype(f32)
    dz = d_gated * y_slope_ref[...].astype(f32)
    dy_low = dy.astype(low)
    normed = (gated * r_col).astype(low)
    out_grad = mm(normed, both_ref[:, D : 2 * D], TN)
    for d in range(8):
        total_ref[d, 192:216] += out_grad[24 * d : 24 * d + 24, 0:PAD]
        total_ref[d, 216:240] += out_grad[24 * d : 24 * d + 24, PAD:D]

    t = lax.broadcasted_iota(jnp.int32, (CHUNK, CHUNK), 0)
    s = lax.broadcasted_iota(jnp.int32, (CHUNK, CHUNK), 1)
    earlier = (t < s).astype(low)
    blank = jnp.zeros((8 - OWN, CHUNK), f32)
    row_head = lax.broadcasted_iota(jnp.int32, (8, WIDE), 0)
    lane = lax.broadcasted_iota(jnp.int32, (8, WIDE), 1)
    by_head = ((lane >= 64 * row_head) & (lane < 64 * row_head + 64)).astype(low)

    chunks = range(GROUP)
    d_scores_all, d_steps_all, inside_all, mixing_all, flow_all = [], [], [], [], []
    entries = [per_head([c[:, 8 + h : 9 + h] for h in range(OWN)]) for c in cols]
    leavings = [per_head([c[:, 16 + h : 17 + h] for h in range(OWN)]) for c in cols]
    wholes = [per_head([whole[8 * j + h : 8 * j + h + 1] for h in range(OWN)]) for j in chunks]
    scores_all = [mm(part(c_low, j), part(b_low, j), NT) for j in chunks]
    d_mixing_all = [mm(part(dy_low, j), stacked(part(x_low, j)), NT) for j in chunks]
    dy_entries = [entries[j] * part(dy, j) for j in chunks]
    to_state = [mm(part(c_low, j), dy_entries[j].astype(low), TN) for j in chunks]
    for j in chunks:
        col = cols[j]
        bar = barred(col, rows_ref[j, 0:1, :])
        scores, d_mixing = scores_all[j], d_mixing_all[j]
        d_scores = jnp.zeros((CHUNK, CHUNK), f32)
        mixings, flows, d_steps = [], [], []
        for h in range(OWN):
            i = 8 * j + h
            decay = jnp.exp(col[:, h : h + 1] - cum[i : i + 1] + bar)
            stepped = decay * step[i : i + 1]
            mixing = scores * stepped
            mixings.append(mixing.astype(low))
            d_mix = d_mixing[:, CHUNK * h : CHUNK * h + CHUNK]
            d_scores = d_scores + d_mix * stepped
            flows.append((d_mix * mixing).astype(low))
            d_steps.append(jnp.sum(d_mix * scores * decay, axis=0, keepdims=True))
        d_scores_all.append(d_scores.astype(low))
        d_steps_all += d_steps + [blank]
        mixing_all.append(jnp.concatenate(mixings, axis=0))
        flow_all.append(jnp.concatenate(flows, axis=0))
    reach_all = [mm(flow_all[j], earlier) for j in chunks]
    dx_in = [mm(mixing_all[j], stacked(part(dy_low, j)), TN) for j in chunks]
    for j in chunks:
        inside_all += [
            jnp.sum(jnp.where(t >= s, part(reach_all[j], h), 0.0), axis=0, keepdims=True)
            for h in range(OWN)
        ] + [blank]

    laters = [None] * GROUP
    later = state_ref[...]
    for j in reversed(range(GROUP)):
        laters[j] = later
        later = wholes[j] * later + to_state[j]
    state_ref[...] = later

    bs = [part(b_low, j) for j in chunks]
    cs = [part(c_low, j) for j in chunks]
    states = [kept_ref[j] for j in chunks]
    state_lows = [a.astype(low) for a in states]
    later_lows = [a.astype(low) for a in laters]
    from_laters = [mm(bs[j], later_lows[j]) for j in chunks]
    from_states = [mm(cs[j], state_lows[j]) for j in chunks]
    dc_in = [mm(d_scores_all[j], bs[j]) for j in chunks]
    db_in = [mm(d_scores_all[j], cs[j], TN) for j in chunks]
    dc_out = [mm(dy_entries[j].astype(low), state_lows[j], NT) for j in chunks]
    db_out = [
        mm((leavings[j] * part(x, j)).astype(low), later_lows[j], NT) for j in chunks
    ]
    xv = [mm(by_head, (part(x, j) * from_laters[j]).astype(low), NT) for j in chunks]
    row_state = [mm(by_head, (dy_entries[j] * from_states[j]).astype(low), NT) for j in chunks]
    overlap = [
        jnp.sum(mm(by_head, (laters[j] * states[j]).astype(low), NT), axis=1, keepdims=True)
        for j in chunks
    ]
    dxs = [dx_in[j] + leavings[j] * from_laters[j] for j in chunks]
    dcs = [dc_in[j] + dc_out[j] for j in chunks]
    dbs = [db_in[j] + db_out[j] for j in chunks]
    stack = lambda a: jnp.concatenate(a, axis=0)
    ended = to_end * stack(xv)
    col_state = ended * step
    d_step = stack(d_steps_all) + ended
    d_ld = (
        stack(inside_all)
        + reaching(stack(row_state), col_state)
        + whole * stack(overlap)
    )
    d_dt = (d_step - d_ld * ea) * jax.nn.sigmoid(v)
    head_grad_ref[0] += sum([eight(d_dt, j) for j in range(GROUP)])
    head_grad_ref[1] += sum([eight(d_ld * ld, j) for j in range(GROUP)])
    skip_grad_ref[...] += jnp.sum((dy * x).reshape(BLOCK // 8, 8, WIDE), axis=0)

    dx = stack(dxs) + skip_ref[...] * dy
    later_ref[0:BLOCK, 0:WIDE] = dx * slope_ref[:, :WIDE].astype(f32)
    later_ref[0:BLOCK, WIDE:256] = jnp.zeros((BLOCK, 256 - WIDE), f32)
    later_ref[0:BLOCK, 256:384] = stack(dbs) * slope_ref[:, 256:384].astype(f32)
    later_ref[0:BLOCK, 384:512] = stack(dcs) * slope_ref[:, 384:512].astype(f32)
    d_conv_in = jnp.zeros((BLOCK, 512), f32)
    for k in range(CONV):
        moved = later_ref[pl.ds(CONV - 1 - k, BLOCK), :]
        d_conv_in = d_conv_in + conv_ref[k : k + 1, :] * moved
        conv_grad_ref[k] += jnp.sum((moved * conv_in).reshape(BLOCK // 8, 8, 512), axis=0)
        if k == CONV - 1:
            conv_grad_ref[CONV] += jnp.sum(moved.reshape(BLOCK // 8, 8, 512), axis=0)

    turned = []
    for j in range(GROUP):
        tall = [jnp.zeros((64, CHUNK), f32), eight(d_dt, j), jnp.zeros((56, CHUNK), f32)]
        turned.append(jnp.concatenate(tall, axis=0).T)
    d_proj_ref[:, 0:128] = dz[:, 0:128].astype(low)
    d_proj_ref[:, 128:256] = jnp.concatenate(
        [dz[:, 128:WIDE], stack(turned)[:, 64:128]], axis=1
    ).astype(low)
    d_proj_ref[:, 256:PAD] = d_conv_in.astype(low)

    in_grad = mm(both_ref[:, 0:D], d_proj_ref[...], TN)
    for d in range(8):
        total_ref[d, 0:192] += in_grad[192 * d : 192 * d + 192]
    given_ref[...] = mm(d_proj_ref[...], w_ref[...], NT).astype(low)

    row = count - 1 - step_id
    up = lax.rem(row - place_ref[1] + 4, 4)
    for k, ref in enumerate((top_0, top_1, top_2, top_3)):

        @pl.when(up == k)
        def _():
            for j in range(GROUP):
                ref[j] = given_ref[CHUNK * j : CHUNK * j + 64, :]

    for k, ref in enumerate((bottom_0, bottom_1, bottom_2, bottom_3)):
        for j in range(GROUP):

            @pl.when(lax.rem(j - place_ref[0] + 4, 4) == k)
            def _():
                ref[row] = given_ref[CHUNK * j + 64 : CHUNK * (j + 1), :]

    @pl.when(step_id == count - 1)
    def _():
        lane = lax.broadcasted_iota(jnp.int32, (8, 256), 1)
        head = lax.broadcasted_iota(jnp.int32, (8, 256), 0)
        bias = jnp.sum(head_grad_ref[0], axis=1, keepdims=True)
        rate = jnp.sum(head_grad_ref[1], axis=1, keepdims=True)
        own = lax.broadcasted_iota(jnp.int32, (8, WIDE), 0) * HEADDIM
        of_head = lax.broadcasted_iota(jnp.int32, (8, WIDE), 1) - own
        skips = jnp.sum(skip_grad_ref[...], axis=0, keepdims=True)
        skips = jnp.where((of_head >= 0) & (of_head < HEADDIM), skips, 0.0)
        skips = jnp.sum(skips, axis=1, keepdims=True)
        heads = jnp.zeros((8, 256), f32)
        for q, value in enumerate((bias, rate, skips)):
            at = 9 * place_ref[2] + OWN * q + head
            high = value.astype(low).astype(f32)
            rest = (value - high).astype(low).astype(f32)
            heads = heads + jnp.where((lane == at) & (head < OWN), high, 0.0)
            heads = heads + jnp.where((lane == at + 72) & (head < OWN), rest, 0.0)
        taps = [jnp.sum(conv_grad_ref[k], axis=0, keepdims=True) for k in range(CONV + 1)]
        for k in range(CONV):
            sums_ref[k : k + 1, 0:512] = taps[k]
        sums_ref[0:1, 512:PAD] = taps[CONV][:, 0:256]
        sums_ref[1:2, 512:PAD] = taps[CONV][:, 256:512]
        sums_ref[2:3, 512:PAD] = jnp.zeros((1, 256), f32)
        sums_ref[3:4, 512:PAD] = jnp.sum(heads, axis=0, keepdims=True)
        high = sums_ref[0:4, :].astype(low).astype(f32)
        tail = jnp.concatenate([high, sums_ref[0:4, :] - high], axis=0)
        for d in range(8):
            own = jnp.concatenate([total_ref[d], tail], axis=0).astype(low)

            @pl.when(lax.rem(place_ref[2], 2) == d % 2)
            def _():
                grads_ref[d // 2] = own

            @pl.when(lax.rem(place_ref[2], 2) != d % 2)
            def _():
                others_ref[d // 2] = own


def ssd_forward(both, w, w_out, rows, conv, heads, skip):
    length = both.shape[0]
    steps = length // BLOCK
    whole = lambda shape: pl.BlockSpec(shape, lambda i: (0,) * len(shape))
    here = lambda width: pl.BlockSpec((BLOCK, width), lambda i: (i, 0))
    return pl.pallas_call(
        forward_kernel,
        grid=(steps,),
        in_specs=[
            here(2 * D),
            whole((D, PAD)),
            whole((WIDE, D)),
            pl.BlockSpec((GROUP, 8, CHUNK), lambda i: (i, 0, 0)),
            whole((8, 512)),
            whole((2, 8 * GROUP, CHUNK)),
            whole((1, WIDE)),
        ],
        out_specs=[
            here(PAD),
            here(512),
            here(512),
            here(WIDE),
            here(WIDE),
            here(WIDE),
            here(WIDE),
            pl.BlockSpec((GROUP, STATE, WIDE), lambda i: (i, 0, 0)),
            pl.BlockSpec((GROUP, 1, CHUNK, D), lambda i: (0, i, 0, 0)),
            pl.BlockSpec((8, BLOCK), lambda i: (0, i)),
        ],
        out_shape=[
            jax.ShapeDtypeStruct((length, PAD), low),
            jax.ShapeDtypeStruct((length, 512), low),
            jax.ShapeDtypeStruct((length, 512), low),
            jax.ShapeDtypeStruct((length, WIDE), low),
            jax.ShapeDtypeStruct((length, WIDE), low),
            jax.ShapeDtypeStruct((length, WIDE), low),
            jax.ShapeDtypeStruct((length, WIDE), f32),
            jax.ShapeDtypeStruct((length // CHUNK, STATE, WIDE), f32),
            jax.ShapeDtypeStruct((GROUP, steps, CHUNK, D), low),
            jax.ShapeDtypeStruct((8, length), f32),
        ],
        scratch_shapes=[pltpu.VMEM((BLOCK + 8, 512), f32), pltpu.VMEM((STATE, WIDE), f32)],
        compiler_params=pltpu.CompilerParams(
            dimension_semantics=("arbitrary",), vmem_limit_bytes=56 * 1024 * 1024
        ),
        name="ssd_forward",
    )(both, w, w_out, rows, conv, heads, skip)


def ssd_backward(place, both, w, proj, rows, conv, heads, skip, *saved):
    length = proj.shape[0]
    steps = length // BLOCK
    back = lambda i: steps - 1 - i
    whole = lambda shape: pl.BlockSpec(shape, lambda i: (0,) * len(shape))
    here = lambda width: pl.BlockSpec((BLOCK, width), lambda i: (back(i), 0))
    return pl.pallas_call(
        backward_kernel,
        grid=(steps,),
        in_specs=[
            pl.BlockSpec(memory_space=pltpu.SMEM),
            here(PAD),
            whole((D, PAD)),
            here(2 * D),
            pl.BlockSpec((GROUP, 8, CHUNK), lambda i: (back(i), 0, 0)),
            whole((8, 512)),
            whole((2, 8 * GROUP, CHUNK)),
            whole((1, WIDE)),
            here(512),
            here(512),
            here(WIDE),
            here(WIDE),
            here(WIDE),
            here(WIDE),
            pl.BlockSpec((GROUP, STATE, WIDE), lambda i: (back(i), 0, 0)),
        ],
        out_specs=[
            *[whole((4, 64, D)) for _ in range(8)],
            whole((4, 248, PAD)),
            whole((4, 248, PAD)),
        ],
        out_shape=[
            *[jax.ShapeDtypeStruct((4, 64, D), low) for _ in range(8)],
            jax.ShapeDtypeStruct((4, 248, PAD), low),
            jax.ShapeDtypeStruct((4, 248, PAD), low),
        ],
        scratch_shapes=[
            pltpu.VMEM((BLOCK + 8, 512), f32),
            pltpu.VMEM((STATE, WIDE), f32),
            pltpu.VMEM((CONV + 1, 8, 512), f32),
            pltpu.VMEM((2, 8, CHUNK), f32),
            pltpu.VMEM((8, WIDE), f32),
            pltpu.VMEM((BLOCK, PAD), low),
            pltpu.VMEM((BLOCK, D), low),
            pltpu.VMEM((8, 240, PAD), f32),
            pltpu.VMEM((8, PAD), f32),
        ],
        compiler_params=pltpu.CompilerParams(
            dimension_semantics=("arbitrary",), vmem_limit_bytes=56 * 1024 * 1024
        ),
        name="ssd_backward",
    )(place, proj, w, both, rows, conv, heads, skip, *saved)


epsilon = 1e-05
BOTH = ("dp", "seq")
X_GROUPS = [[4 * y + x for x in range(4)] for y in range(4)]
Z_GROUPS = [[2 * z + core for z in range(4)] for core in range(2)]
Y_GROUPS = [[4 * y + x for y in range(4)] for x in range(4)]


def columns_of(a, small):
    rows = a.shape[0]
    z = a[:, :INNER].reshape(rows, 16, WIDE)
    x = a[:, INNER : 2 * INNER].reshape(rows, 16, WIDE)
    bc = jnp.broadcast_to(a[:, None, 2 * INNER : 2 * INNER + 256], (rows, 16, 256))
    dt = a[:, 2 * INNER + 256 :].reshape(rows, 16, OWN)
    blank = lambda n: jnp.zeros((rows, 16, n), a.dtype)
    small = jnp.broadcast_to(small[:, None], (rows, 16, 22))
    return jnp.concatenate([z, dt, blank(61), x, small, blank(42), bc], axis=2).transpose(1, 0, 2)


def padded(a):
    return jnp.concatenate(
        [a[:, :WIDE], jnp.zeros((a.shape[0], 64), a.dtype), a[:, WIDE:]], axis=1
    )


def along_x(a, k):
    return lax.ppermute(a, "seq", [(s, (s // 4) * 4 + (s % 4 + k) % 4) for s in range(16)])


def along_y(a, k):
    return lax.ppermute(a, "seq", [(s, ((s // 4 + k) % 4) * 4 + s % 4) for s in range(16)])


def along_z(a, k):
    return lax.ppermute(a, "dp", [(d, ((d // 2 + k) % 4) * 2 + d % 2) for d in range(8)])


def other_core(a):
    return lax.ppermute(a, "dp", [(d, d ^ 1) for d in range(8)])


def put(buf, piece, *at):
    return lax.dynamic_update_slice(buf, piece, tuple(at) + (0,) * (buf.ndim - len(at)))


def take(a, i):
    return lax.dynamic_index_in_dim(a, i % a.shape[0], 0, False)


def added(a, b):
    return (a.astype(f32) + b.astype(f32)).astype(low)


def ring_sum(block, along, wait):
    h = block[2].shape[0] // 2
    from_up, from_down = wait((along(block[2][:h], 1), along(block[2][h:], 3)))
    up = jnp.concatenate([added(block[1][:h], from_up), block[1][h:]], axis=0)
    down = jnp.concatenate([block[3][:h], added(block[3][h:], from_down)], axis=0)
    up, down = along(up, 1), along(down, 3)
    return block[0].astype(f32) + up.astype(f32) + down.astype(f32)


def scattered_sum(top, bottom):
    me = lax.axis_index("seq")
    x, y = me % 4, me // 4
    total = lambda own, sent: sum([s.astype(f32) for s in sent], own.astype(f32))
    came = []

    def wait(pieces):
        came.extend(pieces)
        return pieces

    top = ring_sum(top, along_y, wait).astype(low)
    bottom = ring_sum(bottom, along_x, wait).astype(low)
    own_top = total(take(top, x), [along_x(take(top, x + k), k) for k in (2, 1, 3)])
    own_bottom = total(take(bottom, y), [along_y(take(bottom, y + k), k) for k in (2, 1, 3)])
    return jnp.concatenate([own_top, own_bottom], axis=0), came


def gathered_z(a):
    d = lax.axis_index("dp")
    z, core = d // 2, d % 2
    h = a.shape[0] // 2
    first, last = a[:h], a[h:]
    up_first = along_z(first, 1)
    down_last = along_z(last, 3)
    up_last = along_z(last, 1)
    down_first = along_z(first, 3)
    far_first = along_z(up_first, 1)
    far_last = along_z(down_last, 3)
    mine = put(jnp.zeros((4, 2, h, a.shape[1]), a.dtype), a.reshape(1, 2, h, -1), z)
    for k, p, q in ((3, up_first, up_last), (1, down_first, down_last), (2, far_first, far_last)):
        mine = put(mine, p[None, None], (z + k) % 4, 0)
        mine = put(mine, q[None, None], (z + k) % 4, 1)
    mine = mine.reshape(4, 1, 2 * h, -1)
    other = other_core(mine)
    first = core == 0
    pair = (jnp.where(first, mine, other), jnp.where(first, other, mine))
    return jnp.concatenate(pair, axis=1).reshape(8, 2 * h, -1)


def seq_sum(a):
    a = a + along_x(a, 1) + along_x(a, 3) + along_x(a, 2)
    return a + along_y(a, 1) + along_y(a, 3) + along_y(a, 2)


def block_order(back):
    pairs = [(f, (f % 8) * 16 + f // 8) for f in range(128)]
    return [(b, a) for a, b in pairs] if back else pairs


def local(
    hidden,
    segments,
    pre_gain,
    w_in,
    conv_weight,
    conv_bias,
    dt_bias,
    a_log,
    d_skip,
    gate_gain,
    w_out,
    grad_out,
):
    me = lax.axis_index("seq")
    row = lax.axis_index("dp")
    tokens = hidden[0].astype(f32)
    r0 = lax.rsqrt(jnp.mean(tokens * tokens, axis=-1, keepdims=True) + epsilon)
    hn = (tokens * r0).astype(low)
    both = jnp.concatenate([hn, grad_out[0]], axis=1)
    both = lax.all_gather(both, "seq", axis=0, tiled=True)

    gain_in = pre_gain.astype(f32)[:, None]
    gain_out = gate_gain.astype(f32)[:, None]
    w_in_wide = w_in.astype(f32)
    w_out_wide = w_out.astype(f32)
    small = jnp.concatenate([conv_weight.reshape(-1), conv_bias, segments[0].astype(low)])
    small = jnp.pad(small, (0, 264 - small.shape[0])).reshape(12, 22)
    parts = columns_of((w_in_wide * gain_in).astype(low), small).reshape(16 * 12, PAD)
    parts = lax.all_to_all(parts, "seq", 0, 0, tiled=True)
    segment = parts[:, 448:470].reshape(16, 264)[:, 130:258].astype(f32).reshape(1, 2048)
    before = jnp.concatenate([jnp.full((1, 1), -1.0, f32), segment[:, :-1]], axis=1)
    blocks = lax.ppermute((w_out_wide * gain_out).astype(low), BOTH, block_order(False))
    weights = gathered_z(jnp.concatenate([parts, blocks.reshape(48, PAD)], axis=0))
    w_own = weights[:, :192].reshape(D, PAD)
    w_out_own = weights[:, 192:].reshape(WIDE, D)
    conv_all = weights[:, :192, 448:470].reshape(128, 264)[:, :130].astype(f32)
    conv_all = conv_all.reshape(128, 5, 26).transpose(1, 0, 2).reshape(5, CONV_CH)
    conv = jnp.concatenate(
        [lax.dynamic_slice_in_dim(conv_all, me * WIDE, WIDE, 1), conv_all[:, INNER:]], axis=1
    )
    conv = jnp.concatenate([padded(conv), jnp.zeros((3, 512), f32)], axis=0)
    own = lambda a: lax.dynamic_slice_in_dim(a, me * OWN, OWN, 0)
    tall = lambda a: jnp.broadcast_to(
        jnp.tile(jnp.pad(own(a), (0, 8 - OWN)), GROUP)[:, None], (8 * GROUP, CHUNK)
    )
    heads = jnp.stack([tall(dt_bias), tall(a_log)])
    skip = jnp.repeat(own(d_skip), 64)[None]
    by_chunk = lambda rows: jnp.concatenate(
        rows + [jnp.zeros((8 - len(rows), 2048), f32)], axis=0
    ).reshape(8, 16, CHUNK).transpose(1, 0, 2)

    proj, *saved, partial_out, sums = ssd_forward(
        both, w_own, w_out_own, by_chunk([segment, before]), conv, heads, skip
    )
    total = lax.psum_scatter(
        partial_out.reshape(2048, D), "seq", scatter_dimension=0, tiled=True, axis_index_groups=X_GROUPS
    )
    sums = seq_sum(sums[:2].reshape(32, 128)).reshape(2, 2048)
    r = lax.rsqrt(sums[0:1] / INNER + epsilon)
    c = r * r * r * (sums[1:2] / INNER)

    place = jnp.stack([me % 4, me // 4, row])
    *pieces, grads, others = ssd_backward(
        place, both, w_own, proj, by_chunk([segment, before, r, c]), conv, heads, skip, *saved
    )
    v, came = scattered_sum(pieces[:4], pieces[4:])
    grads = added(grads, other_core(others)).reshape(4 * 248, PAD)
    grads, total = lax.optimization_barrier((grads, total))
    grads = lax.psum_scatter(
        grads, "dp", scatter_dimension=0, tiled=True, axis_index_groups=Z_GROUPS
    )
    grads, total = lax.optimization_barrier((grads, total))
    total = lax.psum_scatter(
        total, "seq", scatter_dimension=0, tiled=True, axis_index_groups=Y_GROUPS
    )
    small = (grads[240:244].astype(f32) + grads[244:248].astype(f32)).astype(low)
    g_parts = jnp.concatenate(
        [grads[:192].reshape(16, 12, PAD), jnp.broadcast_to(small[None], (16, 4, PAD))], axis=1
    )
    g_parts = lax.all_to_all(g_parts, "seq", 0, 0)
    g_out = lax.ppermute(grads[192:240], BOTH, block_order(True)).astype(f32)
    g_out = jnp.concatenate([g_out[:24], g_out[24:]], axis=1)
    small = g_parts[:, 12:].astype(f32)
    g_parts = g_parts[:, :12]
    conv_sum = jnp.concatenate(
        [
            small[:, :, :WIDE].transpose(1, 0, 2).reshape(CONV, INNER),
            jnp.sum(small[:, :, 256:512], axis=0),
        ],
        axis=1,
    )
    bias_sum = jnp.concatenate(
        [small[:, 0, 512 : 512 + WIDE].reshape(INNER), jnp.sum(small[:, 1, 512:], axis=0)]
    )
    at = 26 * (16 * row + me)
    conv_sum = lax.dynamic_slice_in_dim(conv_sum, at, 26, 1)
    bias_sum = lax.dynamic_slice_in_dim(bias_sum, at, 26, 0)
    head_sum = small[:, 3, 512:656].reshape(16, 16, 3, OWN).sum(axis=1)
    head_sum = head_sum.transpose(1, 0, 2).reshape(3, HEADS)
    g_parts = g_parts.astype(f32).transpose(1, 0, 2)
    g_in = jnp.concatenate(
        [
            g_parts[:, :, :WIDE].reshape(12, INNER),
            g_parts[:, :, 256 : 256 + WIDE].reshape(12, INNER),
            jnp.sum(g_parts[:, :, 512:], axis=1),
            g_parts[:, :, WIDE : WIDE + OWN].reshape(12, HEADS),
        ],
        axis=1,
    )
    grad_w_in = gain_in * g_in
    grad_pre_gain = jnp.sum(w_in_wide * g_in, axis=1)
    grad_w_out = gain_out * g_out
    grad_gate_gain = jnp.sum(w_out_wide * g_out, axis=1)
    r_own = lax.dynamic_slice_in_dim(r[0], me * 128, 128, 0)
    block_out = (r_own[:, None] * total.astype(f32) + tokens).astype(low)
    mean = jnp.mean(v * tokens, axis=-1, keepdims=True)
    grad_hidden = (
        grad_out[0].astype(f32) + r0 * v - tokens * (r0 * r0 * r0 * mean)
    ).astype(low)
    return (
        block_out[None],
        grad_hidden[None],
        grad_pre_gain,
        grad_w_in,
        conv_sum,
        bias_sum,
        head_sum[0],
        head_sum[1],
        head_sum[2],
        grad_gate_gain,
        grad_w_out,
    )


def solution(mesh):
    placed = (
        P("dp", "seq", None),
        P("dp", "seq"),
        P(BOTH),
        P(BOTH, None),
        P(None, BOTH),
        P(BOTH),
        P(),
        P(),
        P(),
        P(BOTH),
        P(BOTH, None),
        P("dp", "seq", None),
    )
    return jax.shard_map(
        local,
        mesh=mesh,
        in_specs=placed,
        out_specs=(
            P("dp", "seq", None),
            P("dp", "seq", None),
            P(BOTH),
            P(BOTH, None),
            P(None, BOTH),
            P(BOTH),
            P(),
            P(),
            P(),
            P(BOTH),
            P(BOTH, None),
        ),
        check_vma=False,
    )
```
